32 devices in a mesh: seq: 8 (over z, x), blk: 4 (over y, core).
Axes of the slice: x: 2, y: 2, z: 4, core: 2. Of those that a mesh axis runs over, the one named last changes fastest.
Arguments:
- qkv: bfloat16 [4096, 3072], P(('seq', 'blk')), may hold values from -24 to 24
- kept_kv: bfloat16 [16, 2, 128, 1024], P('blk', None, None, 'seq'), may hold values from -24 to 24
- cur_list: int32 [32, 2], replicated, may hold values from 0 to 31, as said below
- kept_list: int32 [32, 12], replicated, may hold values from 0 to 15, as said below
- kept_count: int32 [32], replicated, may hold values from 1 to 12, as said below
Outputs:
- attn_out: bfloat16 [4096, 1024], P(('seq', 'blk'))
The draws below stay inside these ranges and needn't reach their ends.
Inputs may be any that keep to these rules, and one draw needn't show every extreme that they name: `cur_list`: row t lists 2 different tiles t2 of tile t's spatial region, that is with (t2) % 4 equal to (t) % 4; the first entry is t itself. `kept_list`: each row names 12 different kept blocks. `kept_count`: some tile uses all 12 slots.
All inputs are finite; a program needn't handle non-finite values.
Results may differ from the reference program's by a relative error of at most 0.0025.
Values may be sent and summed in bfloat16 or wider, within the bound.
No kernel may reach another device: no remote copies, remote signals or barrier semaphores. Data moves between devices by JAX's collectives and lax.ppermute only.
A program may use at most 64 MiB of HBM per device.

```python
import math
import jax
import jax.numpy as jnp
from jax import lax

HEAD_DIM = 128
HEADS = 8
TILE = 128
TILES_DEV = 1
REGIONS = 4
REGION_TILES = 8
TILES = 32
TOKENS = 4096
CUR_BLOCKS = 2
KEPT = 16
WINDOW = 12


def draw_qkv(key, part):
    key_base, key_scale = jax.random.split(key, 2)
    shape = (TOKENS, 3, HEADS * HEAD_DIM)
    base = jax.random.normal(key_base, shape, jnp.float32)
    log_scale = jax.random.uniform(key_scale, (TOKENS, 3, 1), jnp.float32, math.log(0.3), math.log(3.0))
    is_query = (jnp.arange(3) == 0)[None, :, None]
    factor = jnp.where(is_query, 1.0, jnp.exp(log_scale))
    values = jnp.clip(base * factor, -24.0, 24.0)
    return values.reshape(TOKENS, 3 * HEADS * HEAD_DIM).astype(jnp.bfloat16)


def draw_kept_kv(key, part):
    key_base, key_scale = jax.random.split(key, 2)
    shape = (KEPT, 2, TILE, HEADS * HEAD_DIM)
    base = jax.random.normal(key_base, shape, jnp.float32)
    log_scale = jax.random.uniform(key_scale, (KEPT, 2, TILE, 1), jnp.float32, math.log(0.3), math.log(3.0))
    return jnp.clip(base * jnp.exp(log_scale), -24.0, 24.0).astype(jnp.bfloat16)


def draw_cur_list(key, part):
    tile_keys = jax.random.split(key, TILES)
    tile_ids = jnp.arange(TILES, dtype=jnp.int32)

    def one_tile(tile_key, tile_id):
        own_place = tile_id // TILES_DEV // REGIONS * TILES_DEV + tile_id % TILES_DEV
        region = tile_id // TILES_DEV % REGIONS
        others = (own_place + 1 + jax.random.permutation(tile_key, REGION_TILES - 1)[:CUR_BLOCKS - 1]) % REGION_TILES
        places = jnp.concatenate([own_place[None], others.astype(jnp.int32)])
        return (places // TILES_DEV * REGIONS + region) * TILES_DEV + places % TILES_DEV
    return jax.vmap(one_tile)(tile_keys, tile_ids).astype(jnp.int32)


def draw_kept_list(key, part):
    tile_keys = jax.random.split(key, TILES)
    return jax.vmap(lambda tile_key: jax.random.permutation(tile_key, KEPT)[:WINDOW])(tile_keys).astype(jnp.int32)


def draw_kept_count(key, part):
    key_first, key_second, key_full = jax.random.split(key, 3)
    first = jax.random.randint(key_first, (TILES,), 0, WINDOW)
    second = jax.random.randint(key_second, (TILES,), 0, WINDOW)
    counts = 1 + first * second // WINDOW
    full_tile = jax.random.randint(key_full, (), 0, TILES)
    return counts.at[full_tile].set(WINDOW).astype(jnp.int32)


def setup_inputs(seed: int = 0) -> dict:
    streams_of = jax.random.split(jax.random.key(seed), 6)
    return {
        "qkv": draw_qkv(jax.random.fold_in(streams_of[5], 71), 0),
        "kept_kv": draw_kept_kv(jax.random.fold_in(streams_of[5], 71), 0),
        "cur_list": draw_cur_list(jax.random.fold_in(streams_of[5], 71), 0),
        "kept_list": draw_kept_list(jax.random.fold_in(streams_of[5], 71), 0),
        "kept_count": draw_kept_count(jax.random.fold_in(streams_of[5], 71), 0),
    }


MASKED_SCORE = -1e+30

def reference(qkv, kept_kv, cur_list, kept_list, kept_count):
    tiles_all = qkv.reshape(TILES, TILE, 3, HEADS, HEAD_DIM)
    kept_all = kept_kv.reshape(KEPT, 2, TILE, HEADS, HEAD_DIM)
    score_scale = 1.0 / math.sqrt(HEAD_DIM)

    def one_tile(inputs):
        tile_index, cur_sel, kept_sel, slot_count = inputs
        own_tile = lax.dynamic_index_in_dim(tiles_all, tile_index, 0, keepdims=False)
        queries = own_tile[:, 0].astype(jnp.float32)
        near_blocks = tiles_all[cur_sel]
        far_blocks = kept_all[kept_sel]
        keys = jnp.concatenate([near_blocks[:, :, 1].reshape(-1, HEADS, HEAD_DIM), far_blocks[:, 0].reshape(-1, HEADS, HEAD_DIM)], 0).astype(jnp.float32)
        values = jnp.concatenate([near_blocks[:, :, 2].reshape(-1, HEADS, HEAD_DIM), far_blocks[:, 1].reshape(-1, HEADS, HEAD_DIM)], 0).astype(jnp.float32)
        is_live = jnp.concatenate([jnp.ones((CUR_BLOCKS * TILE,), dtype=bool), jnp.repeat(jnp.arange(WINDOW) < slot_count, TILE)])
        scores = jnp.einsum('ihd,khd->hik', queries, keys) * score_scale
        scores = jnp.where(is_live, scores, MASKED_SCORE)
        row_max = scores.max(axis=-1, keepdims=True)
        weights = jnp.where(is_live, jnp.exp(scores - row_max), 0.0)
        row_total = weights.sum(axis=-1)
        rounded = lax.optimization_barrier(weights.astype(jnp.bfloat16)).astype(jnp.float32)
        mixture = jnp.einsum('hik,khd->ihd', rounded, values)
        result = mixture / jnp.transpose(row_total)[:, :, None]
        return result.astype(jnp.bfloat16).reshape(TILE, HEADS * HEAD_DIM)
    tile_indices = jnp.arange(TILES, dtype=jnp.int32)
    output = lax.map(one_tile, (tile_indices, cur_list, kept_list, kept_count))
    return output.reshape(TOKENS, HEADS * HEAD_DIM)
```

```python
import functools
import math

import jax
import jax.numpy as jnp
from jax import lax
from jax.experimental import pallas as pl
from jax.experimental.pallas import tpu as pltpu
from jax.sharding import PartitionSpec as P

HEAD_DIM = 128
MASKED_SCORE = -1e30
CHUNK = 4
VMEM_BYTES = 40 * 1024 * 1024


def pack_kernel(qkv_ref, out_ref):
    dests, groups, _, width = out_ref.shape
    for dest in range(dests):
        for group in range(groups):
            start = (group * dests + dest) * width
            out_ref[dest, group] = qkv_ref[:, start : start + width]


def unpack_kernel(parts_ref, out_ref):
    sources, _, width = parts_ref.shape
    for source in range(sources):
        out_ref[:, source * width : (source + 1) * width] = parts_ref[source]


def attention_kernel(
    blk_count,
    tile_len,
    place_ref,
    cur_ref,
    kept_list_ref,
    kept_count_ref,
    span_hbm,
    *refs,
):
    kept_hbm = refs[:blk_count]
    out_ref, span, kept, scores, span_sem, kept_sem = refs[blk_count:]
    sources, _, tok_rows, width = span.shape
    tiles_dev = tok_rows // tile_len
    heads = width // HEAD_DIM
    kept_dev = kept_hbm[0].shape[0]
    near_count = cur_ref.shape[0]
    window = kept_list_ref.shape[0]
    region = place_ref[0]

    span_copy = pltpu.make_async_copy(span_hbm, span, span_sem)
    span_copy.start()
    kept_copies = []
    for i in range(blk_count):
        start = place_ref[1 + i] * kept_dev
        copy = pltpu.make_async_copy(kept_hbm[i], kept.at[pl.ds(start, kept_dev)], kept_sem.at[i])
        copy.start()
        kept_copies.append(copy)
    for copy in kept_copies:
        copy.wait()
    span_copy.wait()

    scale = 1.0 / math.sqrt(HEAD_DIM)
    chunks = [range(i, min(i + CHUNK, window)) for i in range(0, window, CHUNK)]

    def dot_keys(queries, keys):
        return lax.dot_general(
            queries, keys, (((1,), (1,)), ((), ())), preferred_element_type=jnp.float32
        ) * scale

    def one_tile(j, _):
        source = j // tiles_dev
        place = j % tiles_dev
        tile = (source * blk_count + region) * tiles_dev + place
        rows = pl.ds(pl.multiple_of(place * tile_len, tile_len), tile_len)
        count = kept_count_ref[tile]
        near = []
        for c in range(near_count):
            t2 = cur_ref[c, tile]
            near.append((t2 // tiles_dev // blk_count, t2 % tiles_dev))
        near_rows = [(s, pl.ds(pl.multiple_of(p * tile_len, tile_len), tile_len)) for s, p in near]
        far_ids = [kept_list_ref[w, tile] for w in range(window)]
        for h in range(heads):
            cols = slice(h * HEAD_DIM, (h + 1) * HEAD_DIM)
            queries = span[source, 0, rows, cols]

            def far_scores(slots):
                keys = jnp.concatenate([kept[far_ids[w], 0, :, cols] for w in slots], axis=0)
                raw = dot_keys(queries, keys)
                slot = lax.broadcasted_iota(jnp.int32, raw.shape, 1) // tile_len + slots[0]
                return jnp.where(slot < count, raw, MASKED_SCORE)

            def far_values(slots):
                return jnp.concatenate([kept[far_ids[w], 1, :, cols] for w in slots], axis=0)

            def weigh(raw, top, values):
                weights = jnp.exp(raw - top)
                total = jnp.sum(weights, axis=1, keepdims=True)
                mixed = jnp.dot(
                    weights.astype(jnp.bfloat16), values, preferred_element_type=jnp.float32
                )
                return total, mixed

            near_keys = jnp.concatenate([span[s, 1, r, cols] for s, r in near_rows], axis=0)
            near_raw = dot_keys(queries, near_keys)
            first_raw = far_scores(chunks[0])
            top = jnp.maximum(
                jnp.max(near_raw, axis=1, keepdims=True), jnp.max(first_raw, axis=1, keepdims=True)
            )
            for chunk in chunks[1:]:

                def more(top, chunk=chunk):
                    raw = far_scores(chunk)
                    scores[:, chunk[0] * tile_len : (chunk[-1] + 1) * tile_len] = raw
                    return jnp.maximum(top, jnp.max(raw, axis=1, keepdims=True))

                top = lax.cond(chunk[0] < count, more, lambda top: top, top)
            near_values = jnp.concatenate([span[s, 2, r, cols] for s, r in near_rows], axis=0)
            near_total, near_mixed = weigh(near_raw, top, near_values)
            first_total, first_mixed = weigh(first_raw, top, far_values(chunks[0]))
            total, mixed = near_total + first_total, near_mixed + first_mixed
            for chunk in chunks[1:]:

                def add(carry, chunk=chunk):
                    raw = scores[:, chunk[0] * tile_len : (chunk[-1] + 1) * tile_len]
                    more_total, more_mixed = weigh(raw, top, far_values(chunk))
                    return carry[0] + more_total, carry[1] + more_mixed

                total, mixed = lax.cond(
                    chunk[0] < count, add, lambda carry: carry, (total, mixed)
                )
            out_ref[source, rows, cols] = (mixed / total).astype(jnp.bfloat16)
        return 0

    lax.fori_loop(0, sources * tiles_dev, one_tile, 0)


def gather_kept(kept_kv, blk_count):
    me = lax.axis_index("blk")
    if blk_count % 2:
        pieces = [kept_kv]
        origins = [me]
        for d in range(1, blk_count):
            pieces.append(
                lax.ppermute(kept_kv, "blk", [(i, (i + d) % blk_count) for i in range(blk_count)])
            )
            origins.append((me - d) % blk_count)
        return pieces, origins
    pair = [(i, i ^ 1) for i in range(blk_count)]
    pieces, origins = [], []
    for d in range(0, blk_count, 2):
        if d:
            shift = [(i, (i + d) % blk_count) for i in range(blk_count)]
            piece = lax.ppermute(kept_kv, "blk", shift)
        else:
            piece = kept_kv
        pieces += [piece, lax.ppermute(piece, "blk", pair)]
        origins += [(me - d) % blk_count, ((me ^ 1) - d) % blk_count]
    return pieces, origins


def per_device(qkv, kept_kv, cur_list, kept_list, kept_count):
    seq_count = lax.axis_size("seq")
    blk_count = lax.axis_size("blk")
    tok_rows = qkv.shape[0]
    kept_dev, _, tile_len, width = kept_kv.shape
    dtype = qkv.dtype
    vmem = pl.BlockSpec(memory_space=pltpu.VMEM)
    smem = pl.BlockSpec(memory_space=pltpu.SMEM)
    anywhere = pl.BlockSpec(memory_space=pl.ANY)
    params = pltpu.CompilerParams(vmem_limit_bytes=VMEM_BYTES)

    packed = pl.pallas_call(
        pack_kernel,
        out_shape=jax.ShapeDtypeStruct((seq_count, 3, tok_rows, width), dtype),
        in_specs=[vmem],
        out_specs=vmem,
        compiler_params=params,
        name="pack",
    )(qkv)
    span = lax.all_to_all(packed, "seq", split_axis=0, concat_axis=0, tiled=True)
    pieces, origins = gather_kept(kept_kv, blk_count)
    place = jnp.stack([lax.axis_index("blk"), *origins]).astype(jnp.int32)

    attended = pl.pallas_call(
        functools.partial(attention_kernel, blk_count, tile_len),
        out_shape=jax.ShapeDtypeStruct((seq_count, tok_rows, width), dtype),
        in_specs=[smem] * 4 + [anywhere] * (1 + blk_count),
        out_specs=vmem,
        scratch_shapes=[
            pltpu.VMEM((seq_count, 3, tok_rows, width), dtype),
            pltpu.VMEM((blk_count * kept_dev, 2, tile_len, width), dtype),
            pltpu.VMEM((tile_len, kept_list.shape[1] * tile_len), jnp.float32),
            pltpu.SemaphoreType.DMA,
            pltpu.SemaphoreType.DMA((blk_count,)),
        ],
        compiler_params=params,
        name="attention",
    )(place, cur_list.T, kept_list.T, kept_count, span, *pieces)

    returned = lax.all_to_all(attended, "seq", split_axis=0, concat_axis=0, tiled=True)
    return pl.pallas_call(
        unpack_kernel,
        out_shape=jax.ShapeDtypeStruct((tok_rows, seq_count * width), dtype),
        in_specs=[vmem],
        out_specs=vmem,
        compiler_params=params,
        name="unpack",
    )(returned)


def solution(mesh):
    placed = (P(("seq", "blk"), None), P("blk", None, None, "seq"), P(), P(), P())
    return jax.shard_map(
        per_device, mesh=mesh, in_specs=placed, out_specs=P(("seq", "blk"), None), check_vma=False
    )
```

```python
import functools
import math

import jax
import jax.numpy as jnp
from jax import lax
from jax.experimental import pallas as pl
from jax.experimental.pallas import tpu as pltpu
from jax.sharding import PartitionSpec as P

HEAD_DIM = 128
MASKED_SCORE = -1e30
CHUNK = 6
VMEM_BYTES = 40 * 1024 * 1024


def pack_kernel(qkv_ref, out_ref):
    dests, groups, _, width = out_ref.shape
    for dest in range(dests):
        for group in range(groups):
            start = (group * dests + dest) * width
            out_ref[dest, group] = qkv_ref[:, start : start + width]


def unpack_kernel(parts_ref, out_ref):
    sources, _, width = parts_ref.shape
    for source in range(sources):
        out_ref[:, source * width : (source + 1) * width] = parts_ref[source]


def rows_of(place, tile_len):
    return pl.ds(pl.multiple_of(place * tile_len, tile_len), tile_len)


def attention_kernel(blk_count, tile_len, near_count, lists_ref, span, *refs):
    kepts, (out_ref, kept, scores) = refs[:blk_count], refs[blk_count:]
    sources, _, tok_rows, width = span.shape
    tiles_dev = tok_rows // tile_len
    kept_dev = kepts[0].shape[0]
    window = lists_ref.shape[0] - near_count - 1
    unroll = scores.shape[0]
    region = lax.axis_index("blk")

    for step in range(blk_count):
        kept[pl.ds((region ^ step) * kept_dev, kept_dev)] = kepts[step][...]

    factor = math.log2(math.e) / math.sqrt(HEAD_DIM)
    first = range(min(CHUNK, window))
    later = [range(i, min(i + CHUNK, window)) for i in range(CHUNK, window, CHUNK)]

    def stack(pieces):
        return jnp.concatenate(pieces, axis=0)

    def dot_keys(queries, keys):
        raw = lax.dot_general(
            queries, keys, (((1,), (1,)), ((), ())), preferred_element_type=jnp.float32
        )
        return [raw[:, i : i + tile_len] for i in range(0, raw.shape[1], tile_len)]

    def one_group(group, _):
        for head in range(width // HEAD_DIM):
            cols = slice(head * HEAD_DIM, (head + 1) * HEAD_DIM)
            items = []
            for u in range(unroll):
                local = group * unroll + u
                source, place = local // tiles_dev, local % tiles_dev
                tile = (source * blk_count + region) * tiles_dev + place
                near = []
                for c in range(near_count):
                    other = lists_ref[c, tile]
                    near.append(
                        (other // (tiles_dev * blk_count), rows_of(other % tiles_dev, tile_len))
                    )
                far = [lists_ref[near_count + w, tile] for w in range(window)]
                items.append((source, rows_of(place, tile_len), lists_ref[near_count + window, tile], near, far))

            def masked(raws, slots, count):
                return [
                    r if w == 0 else jnp.where(w < count, r, MASKED_SCORE)
                    for w, r in zip(slots, raws)
                ]

            def store(u, start, raws):
                for i, r in enumerate(raws):
                    scores[u, :, (start + i) * tile_len : (start + i + 1) * tile_len] = r

            tops = []
            for u, (source, rows, count, near, far) in enumerate(items):
                keys = [span[s, 1, r, cols] for s, r in near]
                keys += [kept[far[w], 0, :, cols] for w in first]
                raws = dot_keys(span[source, 0, rows, cols], stack(keys))
                raws = raws[:near_count] + masked(raws[near_count:], first, count)
                store(u, 0, raws)
                tops.append(functools.reduce(jnp.maximum, raws))
            for u, (source, rows, count, near, far) in enumerate(items):
                for slots in later:

                    def more(top, u=u, slots=slots):
                        keys = [kept[items[u][4][w], 0, :, cols] for w in slots]
                        raws = dot_keys(span[items[u][0], 0, items[u][1], cols], stack(keys))
                        raws = masked(raws, slots, items[u][2])
                        store(u, near_count + slots[0], raws)
                        return functools.reduce(jnp.maximum, [top, *raws])

                    tops[u] = lax.cond(slots[0] < count, more, lambda top: top, tops[u])
            tops = [jnp.max(top, axis=1, keepdims=True) * factor for top in tops]

            def weigh(u, start, values):
                weights = []
                for i in range(len(values)):
                    r = scores[u, :, (start + i) * tile_len : (start + i + 1) * tile_len]
                    weights.append(jnp.exp2(r * factor - tops[u]))
                rounded = jnp.concatenate([w.astype(jnp.bfloat16) for w in weights], axis=1)
                mixed = jnp.dot(rounded, stack(values), preferred_element_type=jnp.float32)
                return functools.reduce(jnp.add, weights), mixed

            sums = []
            for u, (source, rows, count, near, far) in enumerate(items):
                values = [span[s, 2, r, cols] for s, r in near]
                values += [kept[far[w], 1, :, cols] for w in first]
                sums.append(weigh(u, 0, values))
            for u, (source, rows, count, near, far) in enumerate(items):
                for slots in later:

                    def add(carry, u=u, slots=slots):
                        values = [kept[items[u][4][w], 1, :, cols] for w in slots]
                        total, mixed = weigh(u, near_count + slots[0], values)
                        return carry[0] + total, carry[1] + mixed

                    sums[u] = lax.cond(slots[0] < count, add, lambda carry: carry, sums[u])
            for u, (source, rows, count, near, far) in enumerate(items):
                total = jnp.sum(sums[u][0], axis=1, keepdims=True)
                out_ref[source, rows, cols] = (sums[u][1] / total).astype(jnp.bfloat16)
        return 0

    lax.fori_loop(0, sources * tiles_dev // unroll, one_group, 0)


def swap(array, axis, step):
    if step == 0:
        return array
    count = lax.axis_size(axis)
    return lax.ppermute(array, axis, [(i, i ^ step) for i in range(count)])


def per_device(qkv, kept_kv, cur_list, kept_list, kept_count):
    seq_count = lax.axis_size("seq")
    blk_count = lax.axis_size("blk")
    tok_rows = qkv.shape[0]
    kept_dev, _, tile_len, width = kept_kv.shape
    dtype = qkv.dtype
    tiles = seq_count * (tok_rows // tile_len)
    unroll = math.gcd(tiles, 8)
    near_count, window = cur_list.shape[1], kept_list.shape[1]
    vmem = pl.BlockSpec(memory_space=pltpu.VMEM)
    smem = pl.BlockSpec(memory_space=pltpu.SMEM)
    params = pltpu.CompilerParams(vmem_limit_bytes=VMEM_BYTES)

    lists = jnp.concatenate([cur_list.T, kept_list.T, kept_count[None]], axis=0)
    kepts = [swap(kept_kv, "blk", step) for step in range(blk_count)]
    packed = pl.pallas_call(
        pack_kernel,
        out_shape=jax.ShapeDtypeStruct((seq_count, 3, tok_rows, width), dtype),
        in_specs=[vmem],
        out_specs=vmem,
        compiler_params=params,
        name="pack",
    )(qkv)
    span = lax.all_to_all(packed, "seq", split_axis=0, concat_axis=0, tiled=True)

    attended = pl.pallas_call(
        functools.partial(attention_kernel, blk_count, tile_len, near_count),
        out_shape=jax.ShapeDtypeStruct((seq_count, tok_rows, width), dtype),
        in_specs=[smem] + [vmem] * (1 + blk_count),
        out_specs=vmem,
        scratch_shapes=[
            pltpu.VMEM((blk_count * kept_dev, 2, tile_len, width), dtype),
            pltpu.VMEM((unroll, tile_len, (near_count + window) * tile_len), jnp.float32),
        ],
        compiler_params=params,
        name="attention",
    )(lists, span, *kepts)

    returned = lax.all_to_all(attended, "seq", split_axis=0, concat_axis=0, tiled=True)
    return pl.pallas_call(
        unpack_kernel,
        out_shape=jax.ShapeDtypeStruct((tok_rows, seq_count * width), dtype),
        in_specs=[vmem],
        out_specs=vmem,
        compiler_params=params,
        name="unpack",
    )(returned)


def solution(mesh):
    placed = (P(("seq", "blk"), None), P("blk", None, None, "seq"), P(), P(), P())
    return jax.shard_map(
        per_device, mesh=mesh, in_specs=placed, out_specs=P(("seq", "blk"), None), check_vma=False
    )
```

```python
import functools
import math

import jax
import jax.numpy as jnp
from jax import lax
from jax.experimental import pallas as pl
from jax.experimental.pallas import tpu as pltpu
from jax.sharding import PartitionSpec as P

HEAD_DIM = 128
MASKED_SCORE = -1e30
CHUNK = 6
EARLY = 4
COLLECT_FLOPS = 10**10
VMEM_BYTES = 40 * 1024 * 1024


def pack_kernel(steps, sources, qkv_ref, *refs):
    outs = refs[len(refs) - len(steps) :]
    groups, _, width = outs[0].shape
    me = lax.axis_index("seq")
    for step, out in zip(steps, outs):
        for group in range(groups):
            start = pl.multiple_of((group * sources + (me ^ step)) * width, width)
            out[group] = qkv_ref[:, pl.ds(start, width)]


def merge_kernel(count, *refs):
    for i in range(count):
        refs[-1][i] = refs[i][...]


def collect_kernel(*refs):
    spans, out_ref = refs[:-1], refs[-1]
    me = lax.axis_index("seq")
    for step, span in enumerate(spans):
        out_ref[me ^ step] = span[...]


def unpack_kernel(parts_ref, out_ref):
    sources, _, width = parts_ref.shape
    for source in range(sources):
        out_ref[:, source * width : (source + 1) * width] = parts_ref[source]


def rows_of(place, tile_len):
    return pl.ds(pl.multiple_of(place * tile_len, tile_len), tile_len)


def attention_kernel(blk_count, tile_len, near_count, lists_ref, span, *refs):
    kepts, (out_ref, kept, scores) = refs[:-3], refs[-3:]
    sources, _, tok_rows, width = span.shape
    tiles_dev = tok_rows // tile_len
    kept_dev = kept.shape[0] // blk_count
    window = lists_ref.shape[0] - near_count - 1
    unroll = scores.shape[0]
    region = lax.axis_index("blk")

    pieces = []
    for ref in kepts:
        pieces += [ref] if len(ref.shape) == 4 else [ref.at[i] for i in range(ref.shape[0])]
    for piece, step in zip(pieces, [*range(0, blk_count, 2), *range(1, blk_count, 2)]):
        kept[pl.ds((region ^ step) * kept_dev, kept_dev)] = piece[...]

    factor = math.log2(math.e) / math.sqrt(HEAD_DIM)
    first = range(min(CHUNK, window))
    later = [range(i, min(i + CHUNK, window)) for i in range(CHUNK, window, CHUNK)]

    def stack(pieces):
        return jnp.concatenate(pieces, axis=0)

    def dot_keys(queries, keys):
        raw = lax.dot_general(
            queries, keys, (((1,), (1,)), ((), ())), preferred_element_type=jnp.float32
        )
        return [raw[:, i : i + tile_len] for i in range(0, raw.shape[1], tile_len)]

    def one_group(group, _):
        for head in range(width // HEAD_DIM):
            cols = slice(head * HEAD_DIM, (head + 1) * HEAD_DIM)
            items = []
            for u in range(unroll):
                local = group * unroll + u
                source, place = local // tiles_dev, local % tiles_dev
                tile = (source * blk_count + region) * tiles_dev + place
                near = []
                for c in range(near_count):
                    other = lists_ref[c, tile]
                    near.append(
                        (other // (tiles_dev * blk_count), rows_of(other % tiles_dev, tile_len))
                    )
                far = [lists_ref[near_count + w, tile] for w in range(window)]
                items.append((source, rows_of(place, tile_len), lists_ref[near_count + window, tile], near, far))

            def masked(raws, slots, count):
                return [
                    r if w == 0 else jnp.where(w < count, r, MASKED_SCORE)
                    for w, r in zip(slots, raws)
                ]

            def store(u, start, raws):
                for i, r in enumerate(raws):
                    scores[u, :, (start + i) * tile_len : (start + i + 1) * tile_len] = r

            tops = []
            for u, (source, rows, count, near, far) in enumerate(items):
                keys = [span[s, 1, r, cols] for s, r in near]
                keys += [kept[far[w], 0, :, cols] for w in first]
                raws = dot_keys(span[source, 0, rows, cols], stack(keys))
                raws = raws[:near_count] + masked(raws[near_count:], first, count)
                store(u, 0, raws)
                tops.append(functools.reduce(jnp.maximum, raws))
            for u, (source, rows, count, near, far) in enumerate(items):
                for slots in later:

                    def more(top, u=u, slots=slots):
                        keys = [kept[items[u][4][w], 0, :, cols] for w in slots]
                        raws = dot_keys(span[items[u][0], 0, items[u][1], cols], stack(keys))
                        raws = masked(raws, slots, items[u][2])
                        store(u, near_count + slots[0], raws)
                        return functools.reduce(jnp.maximum, [top, *raws])

                    tops[u] = lax.cond(slots[0] < count, more, lambda top: top, tops[u])
            tops = [jnp.max(top, axis=1, keepdims=True) * factor for top in tops]

            def weigh(u, start, values):
                weights = []
                for i in range(len(values)):
                    r = scores[u, :, (start + i) * tile_len : (start + i + 1) * tile_len]
                    weights.append(jnp.exp2(r * factor - tops[u]))
                rounded = jnp.concatenate([w.astype(jnp.bfloat16) for w in weights], axis=1)
                mixed = jnp.dot(rounded, stack(values), preferred_element_type=jnp.float32)
                return functools.reduce(jnp.add, weights), mixed

            sums = []
            for u, (source, rows, count, near, far) in enumerate(items):
                values = [span[s, 2, r, cols] for s, r in near]
                values += [kept[far[w], 1, :, cols] for w in first]
                sums.append(weigh(u, 0, values))
            for u, (source, rows, count, near, far) in enumerate(items):
                for slots in later:

                    def add(carry, u=u, slots=slots):
                        values = [kept[items[u][4][w], 1, :, cols] for w in slots]
                        total, mixed = weigh(u, near_count + slots[0], values)
                        return carry[0] + total, carry[1] + mixed

                    sums[u] = lax.cond(slots[0] < count, add, lambda carry: carry, sums[u])
            for u, (source, rows, count, near, far) in enumerate(items):
                total = jnp.sum(sums[u][0], axis=1, keepdims=True)
                out_ref[source, rows, cols] = (sums[u][1] / total).astype(jnp.bfloat16)
        return 0

    lax.fori_loop(0, sources * tiles_dev // unroll, one_group, 0)


def swap(array, axis, step):
    if step == 0:
        return array
    count = lax.axis_size(axis)
    return lax.ppermute(array, axis, [(i, i ^ step) for i in range(count)])


def sending_order(count):
    near, far = list(range(1, count // 2)), list(range(count // 2, count))
    return near[:1] + far[:1] + near[1:2] + far[1:] + near[2:]


def per_device(qkv, kept_kv, cur_list, kept_list, kept_count):
    seq_count = lax.axis_size("seq")
    blk_count = lax.axis_size("blk")
    tok_rows = qkv.shape[0]
    kept_dev, _, tile_len, width = kept_kv.shape
    dtype = qkv.dtype
    tiles = seq_count * (tok_rows // tile_len)
    unroll = math.gcd(tiles, 8)
    near_count, window = cur_list.shape[1], kept_list.shape[1]
    vmem = pl.BlockSpec(memory_space=pltpu.VMEM)
    anywhere = pl.BlockSpec(memory_space=pl.ANY)
    smem = pl.BlockSpec(memory_space=pltpu.SMEM)
    params = pltpu.CompilerParams(vmem_limit_bytes=VMEM_BYTES)

    lists = jnp.concatenate([cur_list.T, kept_list.T, kept_count[None]], axis=0)
    kepts = [swap(kept_kv, "blk", step) for step in range(0, blk_count, 2)]
    order = sending_order(seq_count)
    spans = [None] * seq_count
    for steps, before in (([0, *order[:EARLY]], []), (order[EARLY:], kepts[1:])):
        packed = pl.pallas_call(
            functools.partial(pack_kernel, steps, seq_count),
            out_shape=[jax.ShapeDtypeStruct((3, tok_rows, width), dtype)] * len(steps),
            in_specs=[vmem] + [anywhere] * len(before),
            out_specs=[vmem] * len(steps),
            compiler_params=params,
            name="pack",
        )(qkv, *before)
        for step, piece in zip(steps, packed):
            spans[step] = swap(piece, "seq", step)
    after = []
    merged = pl.pallas_call(
        functools.partial(merge_kernel, len(kepts)),
        out_shape=jax.ShapeDtypeStruct((len(kepts), *kept_kv.shape), dtype),
        in_specs=[vmem] * len(kepts) + [anywhere] * len(after),
        out_specs=vmem,
        compiler_params=params,
        name="merge",
    )(*kepts, *after)
    kepts.append(swap(merged, "blk", 1))

    span = pl.pallas_call(
        collect_kernel,
        out_shape=jax.ShapeDtypeStruct((seq_count, 3, tok_rows, width), dtype),
        in_specs=[vmem] * seq_count,
        out_specs=vmem,
        compiler_params=params,
        cost_estimate=pl.CostEstimate(flops=COLLECT_FLOPS, bytes_accessed=0, transcendentals=0),
        name="collect",
    )(*spans)

    attended = pl.pallas_call(
        functools.partial(attention_kernel, blk_count, tile_len, near_count),
        out_shape=jax.ShapeDtypeStruct((seq_count, tok_rows, width), dtype),
        in_specs=[smem] + [vmem] * (1 + len(kepts)),
        out_specs=vmem,
        scratch_shapes=[
            pltpu.VMEM((blk_count * kept_dev, 2, tile_len, width), dtype),
            pltpu.VMEM((unroll, tile_len, (near_count + window) * tile_len), jnp.float32),
        ],
        compiler_params=params,
        name="attention",
    )(lists, span, *kepts)

    returned = lax.all_to_all(attended, "seq", split_axis=0, concat_axis=0, tiled=True)
    return pl.pallas_call(
        unpack_kernel,
        out_shape=jax.ShapeDtypeStruct((tok_rows, seq_count * width), dtype),
        in_specs=[vmem],
        out_specs=vmem,
        compiler_params=params,
        name="unpack",
    )(returned)


def solution(mesh):
    placed = (P(("seq", "blk"), None), P("blk", None, None, "seq"), P(), P(), P())
    return jax.shard_map(
        per_device, mesh=mesh, in_specs=placed, out_specs=P(("seq", "blk"), None), check_vma=False
    )
```

```python
import functools
import math

import jax
import jax.numpy as jnp
from jax import lax
from jax.experimental import pallas as pl
from jax.experimental.pallas import tpu as pltpu
from jax.sharding import PartitionSpec as P

HEAD_DIM = 128
MASKED_SCORE = -1e30
CHUNK = 6
EARLY = 4
GROUP = 8
COLLECT_FLOPS = 10**10
GATHER_FLOPS = 10**10
VMEM_BYTES = 40 * 1024 * 1024


def pack_kernel(steps, sources, qkv_ref, *refs):
    outs = refs[len(refs) - len(steps) :]
    groups, _, width = outs[0].shape
    me = lax.axis_index("seq")
    for step, out in zip(steps, outs):
        for group in range(groups):
            start = pl.multiple_of((group * sources + (me ^ step)) * width, width)
            out[group] = qkv_ref[:, pl.ds(start, width)]


def merge_kernel(count, *refs):
    for i in range(count):
        refs[-1][i] = refs[i][...]


def collect_kernel(*refs):
    spans, out_ref = refs[:-1], refs[-1]
    for step, span in enumerate(spans):
        out_ref[step] = span[1:]


def order_kernel(blk_count, *refs):
    kepts, kept_ref = refs[:-1], refs[-1]
    region = lax.axis_index("blk")
    kept_dev = kept_ref.shape[0] // blk_count
    pieces = []
    for ref in kepts:
        pieces += [ref] if len(ref.shape) == 4 else [ref.at[i] for i in range(ref.shape[0])]
    for piece, step in zip(pieces, [*range(0, blk_count, 2), *range(1, blk_count, 2)]):
        kept_ref[pl.ds((region ^ step) * kept_dev, kept_dev)] = piece[...]


def relay_kernel(passed_ref, *refs):
    count = len(refs) // 2
    for i in range(count):
        refs[count + i][0] = refs[i][...]
        refs[count + i][1] = passed_ref[1 + i]


def gather_kernel(*refs):
    for i, ref in enumerate(refs[:-1]):
        refs[-1][i] = ref[...]


def unpack_kernel(sources, direct, paired, direct_ref, passed_ref, *refs):
    paired_refs, out_ref = refs[:-1], refs[-1]
    width = passed_ref.shape[2]
    me = lax.axis_index("seq")

    def put(step, part):
        out_ref[:, pl.ds(pl.multiple_of((me ^ step) * width, width), width)] = part

    for i, step in enumerate(direct):
        put(step, direct_ref[i])
    put(1, passed_ref[0])
    for step, ref in zip(paired, paired_refs):
        put(step, ref[0])
        put(step + 1, ref[1])


def stack(pieces):
    return jnp.concatenate(pieces, axis=0)


def attend(items, query_refs, span_ref, kept_ref, out_refs, scores, near_count, window):
    tile_len = scores.shape[1]
    factor = math.log2(math.e) / math.sqrt(HEAD_DIM)
    first = range(min(CHUNK, window))
    later = [range(i, min(i + CHUNK, window)) for i in range(CHUNK, window, CHUNK)]

    def dot_keys(queries, keys):
        raw = lax.dot_general(
            queries, keys, (((1,), (1,)), ((), ())), preferred_element_type=jnp.float32
        )
        return [raw[:, i : i + tile_len] for i in range(0, raw.shape[1], tile_len)]

    def masked(raws, slots, count):
        return [r if w == 0 else jnp.where(w < count, r, MASKED_SCORE) for w, r in zip(slots, raws)]

    def queries_of(u):
        step, rows, cols = items[u][:3]
        return query_refs[step][0, rows, cols]

    def far_blocks(u, kind, slots):
        _, _, cols, _, _, far = items[u]
        return [kept_ref[far[w], kind, :, cols] for w in slots]

    def near_blocks(u, kind):
        _, _, cols, _, near, _ = items[u]
        return [span_ref[s, kind, r, cols] for s, r in near]

    def store(u, start, raws):
        for i, r in enumerate(raws):
            scores[u, :, (start + i) * tile_len : (start + i + 1) * tile_len] = r

    def weigh(u, start, values):
        weights = []
        for i in range(len(values)):
            r = scores[u, :, (start + i) * tile_len : (start + i + 1) * tile_len]
            weights.append(jnp.exp2(r * factor - tops[u]))
        rounded = jnp.concatenate([w.astype(jnp.bfloat16) for w in weights], axis=1)
        mixed = jnp.dot(rounded, stack(values), preferred_element_type=jnp.float32)
        return functools.reduce(jnp.add, weights), mixed

    tops = []
    for u, (_, _, _, count, _, _) in enumerate(items):
        raws = dot_keys(queries_of(u), stack(near_blocks(u, 0) + far_blocks(u, 0, first)))
        raws = raws[:near_count] + masked(raws[near_count:], first, count)
        store(u, 0, raws)
        tops.append(functools.reduce(jnp.maximum, raws))
    for u, (_, _, _, count, _, _) in enumerate(items):
        for slots in later:

            def more(top, u=u, slots=slots, count=count):
                raws = dot_keys(queries_of(u), stack(far_blocks(u, 0, slots)))
                raws = masked(raws, slots, count)
                store(u, near_count + slots[0], raws)
                return functools.reduce(jnp.maximum, [top, *raws])

            tops[u] = lax.cond(slots[0] < count, more, lambda top: top, tops[u])
    tops = [jnp.max(top, axis=1, keepdims=True) * factor for top in tops]
    sums = [weigh(u, 0, near_blocks(u, 1) + far_blocks(u, 1, first)) for u in range(len(items))]
    for u, (_, _, _, count, _, _) in enumerate(items):
        for slots in later:

            def add(carry, u=u, slots=slots):
                total, mixed = weigh(u, near_count + slots[0], far_blocks(u, 1, slots))
                return carry[0] + total, carry[1] + mixed

            sums[u] = lax.cond(slots[0] < count, add, lambda carry: carry, sums[u])
    for u, (step, rows, cols, _, _, _) in enumerate(items):
        total = jnp.sum(sums[u][0], axis=1, keepdims=True)
        out_refs[step][rows, cols] = (sums[u][1] / total).astype(jnp.bfloat16)


def attention_kernel(places, blk_count, tile_len, near_count, lists_ref, span_ref, kept_ref, *refs):
    sources = span_ref.shape[0]
    query_refs, buffers, scores = refs[:sources], refs[sources:-1], refs[-1]
    out_refs = [buffers[i] if j is None else buffers[i].at[j] for i, j in places]
    _, _, tok_rows, width = span_ref.shape
    tiles_dev = tok_rows // tile_len
    window = lists_ref.shape[0] - near_count - 1
    me = lax.axis_index("seq")
    region = lax.axis_index("blk")
    items = []
    for step in range(sources):
        for place in range(tiles_dev):
            rows = slice(place * tile_len, (place + 1) * tile_len)
            tile = ((me ^ step) * blk_count + region) * tiles_dev + place
            near = []
            for c in range(near_count):
                other = lists_ref[c, tile]
                source = other // (tiles_dev * blk_count)
                start = pl.multiple_of(other % tiles_dev * tile_len, tile_len)
                near.append((source ^ me, pl.ds(start, tile_len)))
            far = [lists_ref[near_count + w, tile] for w in range(window)]
            count = lists_ref[near_count + window, tile]
            for head in range(width // HEAD_DIM):
                cols = slice(head * HEAD_DIM, (head + 1) * HEAD_DIM)
                items.append((step, rows, cols, count, near, far))

    for start in range(0, len(items), GROUP):
        attend(
            items[start : start + GROUP],
            query_refs,
            span_ref,
            kept_ref,
            out_refs,
            scores,
            near_count,
            window,
        )


def swap(array, axis, step):
    if step == 0:
        return array
    count = lax.axis_size(axis)
    return lax.ppermute(array, axis, [(i, i ^ step) for i in range(count)])


def sending_order(count):
    near, far = list(range(1, count // 2)), list(range(count // 2, count))
    return near[:1] + far[:1] + near[1:2] + far[1:] + near[2:]


def per_device(qkv, kept_kv, cur_list, kept_list, kept_count):
    seq_count = lax.axis_size("seq")
    blk_count = lax.axis_size("blk")
    tok_rows = qkv.shape[0]
    kept_dev, _, tile_len, width = kept_kv.shape
    dtype = qkv.dtype
    near_count, window = cur_list.shape[1], kept_list.shape[1]
    vmem = pl.BlockSpec(memory_space=pltpu.VMEM)
    anywhere = pl.BlockSpec(memory_space=pl.ANY)
    smem = pl.BlockSpec(memory_space=pltpu.SMEM)
    params = pltpu.CompilerParams(vmem_limit_bytes=VMEM_BYTES)

    lists = jnp.concatenate([cur_list.T, kept_list.T, kept_count[None]], axis=0)
    kepts = [swap(kept_kv, "blk", step) for step in range(0, blk_count, 2)]
    order = sending_order(seq_count)
    spans = [None] * seq_count
    for steps, before in (([0, *order[:EARLY]], []), (order[EARLY:], kepts[1:])):
        packed = pl.pallas_call(
            functools.partial(pack_kernel, steps, seq_count),
            out_shape=[jax.ShapeDtypeStruct((3, tok_rows, width), dtype)] * len(steps),
            in_specs=[vmem] + [anywhere] * len(before),
            out_specs=[vmem] * len(steps),
            compiler_params=params,
            name="pack",
        )(qkv, *before)
        for step, piece in zip(steps, packed):
            spans[step] = swap(piece, "seq", step)
    after = []
    merged = pl.pallas_call(
        functools.partial(merge_kernel, len(kepts)),
        out_shape=jax.ShapeDtypeStruct((len(kepts), *kept_kv.shape), dtype),
        in_specs=[vmem] * len(kepts) + [anywhere] * len(after),
        out_specs=vmem,
        compiler_params=params,
        name="merge",
    )(*kepts, *after)
    kepts.append(swap(merged, "blk", 1))

    kept = pl.pallas_call(
        functools.partial(order_kernel, blk_count),
        out_shape=jax.ShapeDtypeStruct((blk_count * kept_dev, 2, tile_len, width), dtype),
        in_specs=[vmem] * len(kepts),
        out_specs=vmem,
        compiler_params=params,
        name="order",
    )(*kepts)
    span = pl.pallas_call(
        collect_kernel,
        out_shape=jax.ShapeDtypeStruct((seq_count, 2, tok_rows, width), dtype),
        in_specs=[vmem] * seq_count,
        out_specs=vmem,
        compiler_params=params,
        cost_estimate=pl.CostEstimate(flops=COLLECT_FLOPS, bytes_accessed=0, transcendentals=0),
        name="collect",
    )(*spans)

    half = seq_count // 2
    direct = [0, half + 1, half]
    paired = [step for step in range(seq_count - 2, 0, -2) if step != half]
    passed = [1] + [step + 1 for step in paired]
    places = [None] * seq_count
    for i, step in enumerate(direct + paired):
        places[step] = (1 + i, None)
    for i, step in enumerate(passed):
        places[step] = (0, i)
    one = jax.ShapeDtypeStruct((tok_rows, width), dtype)
    two = jax.ShapeDtypeStruct((2, tok_rows, width), dtype)
    per_step = tok_rows // tile_len * (width // HEAD_DIM)
    sent, *outs = pl.pallas_call(
        functools.partial(attention_kernel, places, blk_count, tile_len, near_count),
        out_shape=[jax.ShapeDtypeStruct((len(passed), tok_rows, width), dtype)]
        + [one] * len(direct + paired),
        in_specs=[smem] + [vmem] * (2 + seq_count),
        out_specs=[vmem] * (1 + len(direct + paired)),
        scratch_shapes=[
            pltpu.VMEM(
                (min(GROUP, seq_count * per_step), tile_len, (near_count + window) * tile_len), jnp.float32
            )
        ],
        compiler_params=params,
        name="attention",
    )(lists, span, kept, *spans)

    sent = swap(sent, "seq", 1)
    outs = outs[:1] + [swap(out, "seq", step) for out, step in zip(outs[1:], direct[1:])] + outs[len(direct):]
    relayed = pl.pallas_call(
        relay_kernel,
        out_shape=[two] * len(paired),
        in_specs=[vmem] * (1 + len(paired)),
        out_specs=[vmem] * len(paired),
        compiler_params=params,
        name="relay",
    )(sent, *outs[len(direct):])
    relayed = [swap(buffer, "seq", step) for buffer, step in zip(relayed, paired)]
    gathered = pl.pallas_call(
        gather_kernel,
        out_shape=jax.ShapeDtypeStruct((len(direct), tok_rows, width), dtype),
        in_specs=[vmem] * len(direct),
        out_specs=vmem,
        compiler_params=params,
        cost_estimate=pl.CostEstimate(flops=GATHER_FLOPS, bytes_accessed=0, transcendentals=0),
        name="gather",
    )(*outs[: len(direct)])
    return pl.pallas_call(
        functools.partial(unpack_kernel, seq_count, direct, paired),
        out_shape=jax.ShapeDtypeStruct((tok_rows, seq_count * width), dtype),
        in_specs=[vmem] * (2 + len(paired)),
        out_specs=vmem,
        compiler_params=params,
        name="unpack",
    )(gathered, sent, *relayed)


def solution(mesh):
    placed = (P(("seq", "blk"), None), P("blk", None, None, "seq"), P(), P(), P())
    return jax.shard_map(
        per_device, mesh=mesh, in_specs=placed, out_specs=P(("seq", "blk"), None), check_vma=False
    )
```

```python
import functools
import math

import jax
import jax.numpy as jnp
from jax import lax
from jax.experimental import pallas as pl
from jax.experimental.pallas import tpu as pltpu
from jax.sharding import PartitionSpec as P

HEAD_DIM = 128
MASKED_SCORE = -1e30
CHUNK = 6
EARLY = 4
GROUP = 8
COLLECT_FLOPS = 10**10
GATHER_FLOPS = 10**10
VMEM_BYTES = 40 * 1024 * 1024


def pack_kernel(steps, sources, qkv_ref, *refs):
    outs = refs[len(refs) - len(steps) :]
    groups, _, width = outs[0].shape
    me = lax.axis_index("seq")
    for step, out in zip(steps, outs):
        for group in range(groups):
            start = pl.multiple_of((group * sources + (me ^ step)) * width, width)
            out[group] = qkv_ref[:, pl.ds(start, width)]


def merge_kernel(count, blk_count, tiles_dev, *refs):
    pieces, (cur_ref, kept_list_ref, kept_count_ref) = refs[:count], refs[count : count + 3]
    merged_ref, lists_ref = refs[-2:]
    for i in range(count):
        merged_ref[i] = pieces[i][...]
    me = lax.axis_index("seq")
    region = lax.axis_index("blk")
    for at in range(lists_ref.shape[0]):
        step, place = at // tiles_dev, at % tiles_dev
        tile = ((me ^ step) * blk_count + region) * tiles_dev + place
        near = [cur_ref[c, tile] for c in range(cur_ref.shape[0])]
        entries = [other // (tiles_dev * blk_count) ^ me for other in near]
        entries += [other % tiles_dev for other in near]
        entries += [kept_list_ref[w, tile] for w in range(kept_list_ref.shape[0])]
        entries.append(kept_count_ref[0, tile])
        for i, entry in enumerate(entries):
            lists_ref[at, i : i + 1] = jnp.full((1, lists_ref.shape[2]), entry, jnp.int32)


def collect_kernel(*refs):
    spans, out_ref = refs[:-1], refs[-1]
    for step, span in enumerate(spans):
        out_ref[step] = span[1:]


def order_kernel(blk_count, *refs):
    kepts, kept_ref = refs[:-1], refs[-1]
    region = lax.axis_index("blk")
    kept_dev = kept_ref.shape[0] // blk_count
    pieces = []
    for ref in kepts:
        pieces += [ref] if len(ref.shape) == 4 else [ref.at[i] for i in range(ref.shape[0])]
    for piece, step in zip(pieces, [*range(0, blk_count, 2), *range(1, blk_count, 2)]):
        kept_ref[pl.ds((region ^ step) * kept_dev, kept_dev)] = piece[...]


def relay_kernel(passed_ref, *refs):
    count = len(refs) // 2
    for i in range(count):
        refs[count + i][0] = refs[i][...]
        refs[count + i][1] = passed_ref[1 + i]


def gather_kernel(*refs):
    for i, ref in enumerate(refs[:-1]):
        refs[-1][i] = ref[...]


def unpack_kernel(sources, direct, paired, direct_ref, passed_ref, *refs):
    paired_refs, out_ref = refs[:-1], refs[-1]
    width = passed_ref.shape[2]
    me = lax.axis_index("seq")

    def put(step, part):
        out_ref[:, pl.ds(pl.multiple_of((me ^ step) * width, width), width)] = part

    for i, step in enumerate(direct):
        put(step, direct_ref[i])
    put(1, passed_ref[0])
    for step, ref in zip(paired, paired_refs):
        put(step, ref[0])
        put(step + 1, ref[1])


def stack(pieces):
    return jnp.concatenate(pieces, axis=0)


def attend(items, query_refs, span_ref, kept_ref, out_refs, scratch, near_count, window):
    scores, tops_ref, totals_ref, mixed_ref = scratch
    tile_len = scores.shape[1]
    factor = math.log2(math.e) / math.sqrt(HEAD_DIM)
    first = range(min(CHUNK, window))
    later = [range(i, min(i + CHUNK, window)) for i in range(CHUNK, window, CHUNK)]

    def dot_keys(queries, keys):
        raw = lax.dot_general(
            queries, keys, (((1,), (1,)), ((), ())), preferred_element_type=jnp.float32
        )
        return [raw[:, i : i + tile_len] for i in range(0, raw.shape[1], tile_len)]

    def masked(raws, slots, count):
        return [r if w == 0 else jnp.where(w < count, r, MASKED_SCORE) for w, r in zip(slots, raws)]

    def queries_of(u):
        step, rows, cols = items[u][:3]
        return query_refs[step][0, rows, cols]

    def far_blocks(u, kind, slots):
        _, _, cols, _, _, far = items[u]
        return [kept_ref[far[w], kind, :, cols] for w in slots]

    def near_blocks(u, kind):
        _, _, cols, _, near, _ = items[u]
        return [span_ref[s, kind, r, cols] for s, r in near]

    def store(u, start, raws):
        for i, r in enumerate(raws):
            scores[u, :, (start + i) * tile_len : (start + i + 1) * tile_len] = r

    def weigh(u, start, top, values):
        weights = []
        for i in range(len(values)):
            r = scores[u, :, (start + i) * tile_len : (start + i + 1) * tile_len]
            weights.append(jnp.exp2(r * factor - top))
        rounded = jnp.concatenate([w.astype(jnp.bfloat16) for w in weights], axis=1)
        mixed = jnp.dot(rounded, stack(values), preferred_element_type=jnp.float32)
        return functools.reduce(jnp.add, weights), mixed

    for u, (_, _, _, count, _, _) in enumerate(items):
        raws = dot_keys(queries_of(u), stack(near_blocks(u, 0) + far_blocks(u, 0, first)))
        raws = raws[:near_count] + masked(raws[near_count:], first, count)
        store(u, 0, raws)
        tops_ref[u] = functools.reduce(jnp.maximum, raws)
    for u, (_, _, _, count, _, _) in enumerate(items):
        for slots in later:

            @pl.when(slots[0] < count)
            def _(u=u, slots=slots, count=count):
                raws = dot_keys(queries_of(u), stack(far_blocks(u, 0, slots)))
                raws = masked(raws, slots, count)
                store(u, near_count + slots[0], raws)
                tops_ref[u] = functools.reduce(jnp.maximum, [tops_ref[u], *raws])

    tops = []
    for u in range(len(items)):
        top = jnp.max(tops_ref[u], axis=1, keepdims=True) * factor
        tops_ref[u] = jnp.broadcast_to(top, tops_ref.shape[1:])
        tops.append(top)
    for u in range(len(items)):
        total, mixed = weigh(u, 0, tops[u], near_blocks(u, 1) + far_blocks(u, 1, first))
        totals_ref[u], mixed_ref[u] = total, mixed
    for u, (_, _, _, count, _, _) in enumerate(items):
        for slots in later:

            @pl.when(slots[0] < count)
            def _(u=u, slots=slots):
                values = far_blocks(u, 1, slots)
                total, mixed = weigh(u, near_count + slots[0], tops_ref[u], values)
                totals_ref[u] += total
                mixed_ref[u] += mixed

    for u, (step, rows, cols, _, _, _) in enumerate(items):
        total = jnp.sum(totals_ref[u], axis=1, keepdims=True)
        out_refs[step][rows, cols] = (mixed_ref[u] / total).astype(jnp.bfloat16)


def attention_kernel(places, tile_len, near_count, window, lists_ref, span_ref, kept_ref, *refs):
    sources = span_ref.shape[0]
    query_refs, buffers, scratch = refs[:sources], refs[sources:-4], refs[-4:]
    out_refs = [buffers[i] if j is None else buffers[i].at[j] for i, j in places]
    _, _, tok_rows, width = span_ref.shape
    tiles_dev = tok_rows // tile_len
    items = []
    for at in range(sources * tiles_dev):
        step, place = at // tiles_dev, at % tiles_dev
        rows = slice(place * tile_len, (place + 1) * tile_len)
        near = []
        for c in range(near_count):
            start = pl.multiple_of(lists_ref[at, near_count + c, 0] * tile_len, tile_len)
            near.append((lists_ref[at, c, 0], pl.ds(start, tile_len)))
        far = [lists_ref[at, 2 * near_count + w, 0] for w in range(window)]
        count = lists_ref[at, 2 * near_count + window, 0]
        for head in range(width // HEAD_DIM):
            cols = slice(head * HEAD_DIM, (head + 1) * HEAD_DIM)
            items.append((step, rows, cols, count, near, far))

    for start in range(0, len(items), GROUP):
        attend(
            items[start : start + GROUP],
            query_refs,
            span_ref,
            kept_ref,
            out_refs,
            scratch,
            near_count,
            window,
        )


def swap(array, axis, step):
    if step == 0:
        return array
    count = lax.axis_size(axis)
    return lax.ppermute(array, axis, [(i, i ^ step) for i in range(count)])


def sending_order(count):
    near, far = list(range(1, count // 2)), list(range(count // 2, count))
    return near[:1] + far[:1] + near[1:2] + far[1:] + near[2:]


def per_device(qkv, kept_kv, cur_list, kept_list, kept_count):
    seq_count = lax.axis_size("seq")
    blk_count = lax.axis_size("blk")
    tok_rows = qkv.shape[0]
    kept_dev, _, tile_len, width = kept_kv.shape
    dtype = qkv.dtype
    near_count, window = cur_list.shape[1], kept_list.shape[1]
    vmem = pl.BlockSpec(memory_space=pltpu.VMEM)
    anywhere = pl.BlockSpec(memory_space=pl.ANY)
    smem = pl.BlockSpec(memory_space=pltpu.SMEM)
    params = pltpu.CompilerParams(vmem_limit_bytes=VMEM_BYTES)

    kepts = [swap(kept_kv, "blk", step) for step in range(0, blk_count, 2)]
    order = sending_order(seq_count)
    spans = [None] * seq_count
    for steps, before in (([0, *order[:EARLY]], []), (order[EARLY:], kepts[1:])):
        packed = pl.pallas_call(
            functools.partial(pack_kernel, steps, seq_count),
            out_shape=[jax.ShapeDtypeStruct((3, tok_rows, width), dtype)] * len(steps),
            in_specs=[vmem] + [anywhere] * len(before),
            out_specs=[vmem] * len(steps),
            compiler_params=params,
            name="pack",
        )(qkv, *before)
        for step, piece in zip(steps, packed):
            spans[step] = swap(piece, "seq", step)
    after = []
    tiles_dev = tok_rows // tile_len
    merged, lists = pl.pallas_call(
        functools.partial(merge_kernel, len(kepts), blk_count, tiles_dev),
        out_shape=[
            jax.ShapeDtypeStruct((len(kepts), *kept_kv.shape), dtype),
            jax.ShapeDtypeStruct(
                (seq_count * tiles_dev, 2 * near_count + window + 1, HEAD_DIM), jnp.int32
            ),
        ],
        in_specs=[vmem] * len(kepts) + [smem] * 3,
        out_specs=[vmem] * 2,
        compiler_params=params,
        name="merge",
    )(*kepts, cur_list.T, kept_list.T, kept_count[None])
    kepts.append(swap(merged, "blk", 1))

    kept = pl.pallas_call(
        functools.partial(order_kernel, blk_count),
        out_shape=jax.ShapeDtypeStruct((blk_count * kept_dev, 2, tile_len, width), dtype),
        in_specs=[vmem] * len(kepts),
        out_specs=vmem,
        compiler_params=params,
        name="order",
    )(*kepts)
    span = pl.pallas_call(
        collect_kernel,
        out_shape=jax.ShapeDtypeStruct((seq_count, 2, tok_rows, width), dtype),
        in_specs=[vmem] * seq_count,
        out_specs=vmem,
        compiler_params=params,
        cost_estimate=pl.CostEstimate(flops=COLLECT_FLOPS, bytes_accessed=0, transcendentals=0),
        name="collect",
    )(*spans)

    half = seq_count // 2
    direct = [0, half + 1, half]
    paired = [step for step in range(seq_count - 2, 0, -2) if step != half]
    passed = [1] + [step + 1 for step in paired]
    places = [None] * seq_count
    for i, step in enumerate(direct + paired):
        places[step] = (1 + i, None)
    for i, step in enumerate(passed):
        places[step] = (0, i)
    one = jax.ShapeDtypeStruct((tok_rows, width), dtype)
    two = jax.ShapeDtypeStruct((2, tok_rows, width), dtype)
    per_step = tok_rows // tile_len * (width // HEAD_DIM)
    group = min(GROUP, seq_count * per_step)
    sent, *outs = pl.pallas_call(
        functools.partial(attention_kernel, places, tile_len, near_count, window),
        out_shape=[jax.ShapeDtypeStruct((len(passed), tok_rows, width), dtype)]
        + [one] * len(direct + paired),
        in_specs=[vmem] * (3 + seq_count),
        out_specs=[vmem] * (1 + len(direct + paired)),
        scratch_shapes=[
            pltpu.VMEM((group, tile_len, (near_count + window) * tile_len), jnp.float32),
            *[pltpu.VMEM((group, tile_len, tile_len), jnp.float32)] * 3,
        ],
        compiler_params=params,
        name="attention",
    )(lists, span, kept, *spans)

    sent = swap(sent, "seq", 1)
    outs = outs[:1] + [swap(out, "seq", step) for out, step in zip(outs[1:], direct[1:])] + outs[len(direct):]
    relayed = pl.pallas_call(
        relay_kernel,
        out_shape=[two] * len(paired),
        in_specs=[vmem] * (1 + len(paired)),
        out_specs=[vmem] * len(paired),
        compiler_params=params,
        name="relay",
    )(sent, *outs[len(direct):])
    relayed = [swap(buffer, "seq", step) for buffer, step in zip(relayed, paired)]
    gathered = pl.pallas_call(
        gather_kernel,
        out_shape=jax.ShapeDtypeStruct((len(direct), tok_rows, width), dtype),
        in_specs=[vmem] * len(direct),
        out_specs=vmem,
        compiler_params=params,
        cost_estimate=pl.CostEstimate(flops=GATHER_FLOPS, bytes_accessed=0, transcendentals=0),
        name="gather",
    )(*outs[: len(direct)])
    return pl.pallas_call(
        functools.partial(unpack_kernel, seq_count, direct, paired),
        out_shape=jax.ShapeDtypeStruct((tok_rows, seq_count * width), dtype),
        in_specs=[vmem] * (2 + len(paired)),
        out_specs=vmem,
        compiler_params=params,
        name="unpack",
    )(gathered, sent, *relayed)


def solution(mesh):
    placed = (P(("seq", "blk"), None), P("blk", None, None, "seq"), P(), P(), P())
    return jax.shard_map(
        per_device, mesh=mesh, in_specs=placed, out_specs=P(("seq", "blk"), None), check_vma=False
    )
```

```python
import functools
import math

import jax
import jax.numpy as jnp
from jax import lax
from jax.experimental import pallas as pl
from jax.experimental.pallas import tpu as pltpu
from jax.sharding import PartitionSpec as P

HEAD_DIM = 128
MASKED_SCORE = -1e30
CHUNK = 6
EARLY = 4
GROUP = 8
COLLECT_FLOPS = 10**10
FIRST_FLOPS = 10**10
VMEM_BYTES = 40 * 1024 * 1024


def pack_kernel(steps, sources, qkv_ref, *refs):
    outs = refs[len(refs) - len(steps) :]
    groups, _, width = outs[0].shape
    me = lax.axis_index("seq")
    for step, out in zip(steps, outs):
        for group in range(groups):
            start = pl.multiple_of((group * sources + (me ^ step)) * width, width)
            out[group] = qkv_ref[:, pl.ds(start, width)]


def merge_kernel(count, blk_count, tiles_dev, *refs):
    pieces, (cur_ref, kept_list_ref, kept_count_ref) = refs[:count], refs[count : count + 3]
    merged_ref, lists_ref = refs[-2:]
    for i in range(count):
        merged_ref[i] = pieces[i][...]
    me = lax.axis_index("seq")
    region = lax.axis_index("blk")
    for at in range(lists_ref.shape[0]):
        step, place = at // tiles_dev, at % tiles_dev
        tile = ((me ^ step) * blk_count + region) * tiles_dev + place
        near = [cur_ref[c, tile] for c in range(cur_ref.shape[0])]
        entries = [other // (tiles_dev * blk_count) ^ me for other in near]
        entries += [other % tiles_dev for other in near]
        entries += [kept_list_ref[w, tile] for w in range(kept_list_ref.shape[0])]
        entries.append(kept_count_ref[0, tile])
        for i, entry in enumerate(entries):
            lists_ref[at, i : i + 1] = jnp.full((1, lists_ref.shape[2]), entry, jnp.int32)


def collect_kernel(order, *refs):
    for step, span in zip(order, refs):
        refs[-1][step] = span[1:]


def order_kernel(blk_count, *refs):
    kepts, kept_ref = refs[:-1], refs[-1]
    region = lax.axis_index("blk")
    kept_dev = kept_ref.shape[0] // blk_count
    pieces = []
    for ref in kepts:
        pieces += [ref] if len(ref.shape) == 4 else [ref.at[i] for i in range(ref.shape[0])]
    for piece, step in zip(pieces, [*range(0, blk_count, 2), *range(1, blk_count, 2)]):
        kept_ref[pl.ds((region ^ step) * kept_dev, kept_dev)] = piece[...]


def relay_kernel(passed_ref, *refs):
    count = len(refs) // 2
    for i in range(count):
        refs[count + i][0] = refs[i][...]
        refs[count + i][1] = passed_ref[1 + i]


def write_columns(tiles, out_ref, sems):
    me = lax.axis_index("seq")
    copies = []
    for i, (step, tile) in enumerate(tiles):
        width = tile.shape[1]
        columns = pl.ds(pl.multiple_of((me ^ step) * width, width), width)
        copies.append(pltpu.make_async_copy(tile, out_ref.at[:, columns], sems.at[i]))
        copies[-1].start()
    for copy in copies:
        copy.wait()


def first_kernel(direct, passed_ref, *refs):
    tiles = [(1, passed_ref.at[0]), *zip(direct, refs[:-2])]
    write_columns(tiles, refs[-2], refs[-1])


def last_kernel(paired, begun_ref, *refs):
    tiles = []
    for step, ref in zip(paired, refs[:-2]):
        tiles += [(step, ref.at[0]), (step + 1, ref.at[1])]
    write_columns(tiles, refs[-2], refs[-1])


def stack(pieces):
    return jnp.concatenate(pieces, axis=0)


def attend(items, query_refs, span_ref, kept_ref, out_refs, scratch, near_count, window):
    scores, tops_ref, totals_ref, mixed_ref = scratch
    tile_len = scores.shape[1]
    factor = math.log2(math.e) / math.sqrt(HEAD_DIM)
    first = range(min(CHUNK, window))
    later = [range(i, min(i + CHUNK, window)) for i in range(CHUNK, window, CHUNK)]

    def dot_keys(queries, keys):
        raw = lax.dot_general(
            queries, keys, (((1,), (1,)), ((), ())), preferred_element_type=jnp.float32
        )
        return [raw[:, i : i + tile_len] for i in range(0, raw.shape[1], tile_len)]

    def masked(raws, slots, count):
        return [r if w == 0 else jnp.where(w < count, r, MASKED_SCORE) for w, r in zip(slots, raws)]

    def queries_of(u):
        step, rows, cols = items[u][:3]
        return query_refs[step][0, rows, cols]

    def far_blocks(u, kind, slots):
        _, _, cols, _, _, far = items[u]
        return [kept_ref[far[w], kind, :, cols] for w in slots]

    def near_blocks(u, kind):
        _, _, cols, _, near, _ = items[u]
        return [span_ref[s, kind, r, cols] for s, r in near]

    def store(u, start, raws):
        for i, r in enumerate(raws):
            scores[u, :, (start + i) * tile_len : (start + i + 1) * tile_len] = r

    def weigh(u, start, top, values):
        weights = []
        for i in range(len(values)):
            r = scores[u, :, (start + i) * tile_len : (start + i + 1) * tile_len]
            weights.append(jnp.exp2(r * factor - top))
        rounded = jnp.concatenate([w.astype(jnp.bfloat16) for w in weights], axis=1)
        mixed = jnp.dot(rounded, stack(values), preferred_element_type=jnp.float32)
        return functools.reduce(jnp.add, weights), mixed

    for u, (_, _, _, count, _, _) in enumerate(items):
        raws = dot_keys(queries_of(u), stack(near_blocks(u, 0) + far_blocks(u, 0, first)))
        raws = raws[:near_count] + masked(raws[near_count:], first, count)
        store(u, 0, raws)
        tops_ref[u] = functools.reduce(jnp.maximum, raws)
    for u, (_, _, _, count, _, _) in enumerate(items):
        for slots in later:

            @pl.when(slots[0] < count)
            def _(u=u, slots=slots, count=count):
                raws = dot_keys(queries_of(u), stack(far_blocks(u, 0, slots)))
                raws = masked(raws, slots, count)
                store(u, near_count + slots[0], raws)
                tops_ref[u] = functools.reduce(jnp.maximum, [tops_ref[u], *raws])

    tops = []
    for u in range(len(items)):
        top = jnp.max(tops_ref[u], axis=1, keepdims=True) * factor
        tops_ref[u] = jnp.broadcast_to(top, tops_ref.shape[1:])
        tops.append(top)
    for u in range(len(items)):
        total, mixed = weigh(u, 0, tops[u], near_blocks(u, 1) + far_blocks(u, 1, first))
        totals_ref[u], mixed_ref[u] = total, mixed
    for u, (_, _, _, count, _, _) in enumerate(items):
        for slots in later:

            @pl.when(slots[0] < count)
            def _(u=u, slots=slots):
                values = far_blocks(u, 1, slots)
                total, mixed = weigh(u, near_count + slots[0], tops_ref[u], values)
                totals_ref[u] += total
                mixed_ref[u] += mixed

    for u, (step, rows, cols, _, _, _) in enumerate(items):
        total = jnp.sum(totals_ref[u], axis=1, keepdims=True)
        out_refs[step][rows, cols] = (mixed_ref[u] / total).astype(jnp.bfloat16)


def attention_kernel(places, tile_len, near_count, window, lists_ref, span_ref, kept_ref, *refs):
    sources = span_ref.shape[0]
    query_refs, buffers, scratch = refs[:sources], refs[sources:-4], refs[-4:]
    out_refs = [buffers[i] if j is None else buffers[i].at[j] for i, j in places]
    _, _, tok_rows, width = span_ref.shape
    tiles_dev = tok_rows // tile_len
    items = []
    for at in range(sources * tiles_dev):
        step, place = at // tiles_dev, at % tiles_dev
        rows = slice(place * tile_len, (place + 1) * tile_len)
        near = []
        for c in range(near_count):
            start = pl.multiple_of(lists_ref[at, near_count + c, 0] * tile_len, tile_len)
            near.append((lists_ref[at, c, 0], pl.ds(start, tile_len)))
        far = [lists_ref[at, 2 * near_count + w, 0] for w in range(window)]
        count = lists_ref[at, 2 * near_count + window, 0]
        for head in range(width // HEAD_DIM):
            cols = slice(head * HEAD_DIM, (head + 1) * HEAD_DIM)
            items.append((step, rows, cols, count, near, far))

    for start in range(0, len(items), GROUP):
        attend(
            items[start : start + GROUP],
            query_refs,
            span_ref,
            kept_ref,
            out_refs,
            scratch,
            near_count,
            window,
        )


def swap(array, axis, step):
    if step == 0:
        return array
    count = lax.axis_size(axis)
    return lax.ppermute(array, axis, [(i, i ^ step) for i in range(count)])


def sending_order(count):
    near, far = list(range(1, count // 2)), list(range(count // 2, count))
    return near[:1] + far[:1] + near[1:2] + far[1:2] + near[2:] + far[2:]


def per_device(qkv, kept_kv, cur_list, kept_list, kept_count):
    seq_count = lax.axis_size("seq")
    blk_count = lax.axis_size("blk")
    tok_rows = qkv.shape[0]
    kept_dev, _, tile_len, width = kept_kv.shape
    dtype = qkv.dtype
    near_count, window = cur_list.shape[1], kept_list.shape[1]
    vmem = pl.BlockSpec(memory_space=pltpu.VMEM)
    anywhere = pl.BlockSpec(memory_space=pl.ANY)
    smem = pl.BlockSpec(memory_space=pltpu.SMEM)
    params = pltpu.CompilerParams(vmem_limit_bytes=VMEM_BYTES)

    kepts = [swap(kept_kv, "blk", step) for step in range(0, blk_count, 2)]
    order = sending_order(seq_count)
    spans = [None] * seq_count
    for steps in ([0, *order[:EARLY]], order[EARLY:]):
        before = [] if 0 in steps else [*kepts[1:], spans[order[0]]]
        packed = pl.pallas_call(
            functools.partial(pack_kernel, steps, seq_count),
            out_shape=[jax.ShapeDtypeStruct((3, tok_rows, width), dtype)] * len(steps),
            in_specs=[vmem] + [anywhere] * len(before),
            out_specs=[vmem] * len(steps),
            compiler_params=params,
            name="pack",
        )(qkv, *before)
        for step, piece in zip(steps, packed):
            spans[step] = swap(piece, "seq", step)
    after = []
    tiles_dev = tok_rows // tile_len
    merged, lists = pl.pallas_call(
        functools.partial(merge_kernel, len(kepts), blk_count, tiles_dev),
        out_shape=[
            jax.ShapeDtypeStruct((len(kepts), *kept_kv.shape), dtype),
            jax.ShapeDtypeStruct(
                (seq_count * tiles_dev, 2 * near_count + window + 1, HEAD_DIM), jnp.int32
            ),
        ],
        in_specs=[vmem] * len(kepts) + [smem] * 3,
        out_specs=[vmem] * 2,
        compiler_params=params,
        name="merge",
    )(*kepts, cur_list.T, kept_list.T, kept_count[None])
    kepts.append(swap(merged, "blk", 1))

    kept = pl.pallas_call(
        functools.partial(order_kernel, blk_count),
        out_shape=jax.ShapeDtypeStruct((blk_count * kept_dev, 2, tile_len, width), dtype),
        in_specs=[vmem] * len(kepts),
        out_specs=vmem,
        compiler_params=params,
        name="order",
    )(*kepts)
    span = pl.pallas_call(
        functools.partial(collect_kernel, [0, *order]),
        out_shape=jax.ShapeDtypeStruct((seq_count, 2, tok_rows, width), dtype),
        in_specs=[vmem] * seq_count,
        out_specs=vmem,
        compiler_params=params,
        cost_estimate=pl.CostEstimate(flops=COLLECT_FLOPS, bytes_accessed=0, transcendentals=0),
        name="collect",
    )(*[spans[step] for step in [0, *order]])

    half = seq_count // 2
    direct = [0, half + 1, half]
    paired = [step for step in range(seq_count - 2, 0, -2) if step != half]
    passed = [1] + [step + 1 for step in paired]
    places = [None] * seq_count
    for i, step in enumerate(direct + paired):
        places[step] = (1 + i, None)
    for i, step in enumerate(passed):
        places[step] = (0, i)
    one = jax.ShapeDtypeStruct((tok_rows, width), dtype)
    two = jax.ShapeDtypeStruct((2, tok_rows, width), dtype)
    per_step = tok_rows // tile_len * (width // HEAD_DIM)
    group = min(GROUP, seq_count * per_step)
    sent, *outs = pl.pallas_call(
        functools.partial(attention_kernel, places, tile_len, near_count, window),
        out_shape=[jax.ShapeDtypeStruct((len(passed), tok_rows, width), dtype)]
        + [one] * len(direct + paired),
        in_specs=[vmem] * (3 + seq_count),
        out_specs=[vmem] * (1 + len(direct + paired)),
        scratch_shapes=[
            pltpu.VMEM((group, tile_len, (near_count + window) * tile_len), jnp.float32),
            *[pltpu.VMEM((group, tile_len, tile_len), jnp.float32)] * 3,
        ],
        compiler_params=params,
        name="attention",
    )(lists, span, kept, *spans)

    sent = swap(sent, "seq", 1)
    outs = outs[:1] + [swap(out, "seq", step) for out, step in zip(outs[1:], direct[1:])] + outs[len(direct):]
    relayed = pl.pallas_call(
        relay_kernel,
        out_shape=[two] * len(paired),
        in_specs=[vmem] * (1 + len(paired)),
        out_specs=[vmem] * len(paired),
        compiler_params=params,
        name="relay",
    )(sent, *outs[len(direct):])
    relayed = [swap(buffer, "seq", step) for buffer, step in zip(relayed, paired)]
    whole = jax.ShapeDtypeStruct((tok_rows, seq_count * width), dtype)
    begun = pl.pallas_call(
        functools.partial(first_kernel, direct),
        out_shape=whole,
        in_specs=[vmem] * (1 + len(direct)),
        out_specs=anywhere,
        scratch_shapes=[pltpu.SemaphoreType.DMA((1 + len(direct),))],
        compiler_params=params,
        cost_estimate=pl.CostEstimate(flops=FIRST_FLOPS, bytes_accessed=0, transcendentals=0),
        name="first",
    )(sent, *outs[: len(direct)])
    return pl.pallas_call(
        functools.partial(last_kernel, paired),
        out_shape=whole,
        in_specs=[anywhere] + [vmem] * len(paired),
        out_specs=anywhere,
        scratch_shapes=[pltpu.SemaphoreType.DMA((2 * len(paired),))],
        compiler_params=params,
        input_output_aliases={0: 0},
        name="last",
    )(begun, *relayed)


def solution(mesh):
    placed = (P(("seq", "blk"), None), P("blk", None, None, "seq"), P(), P(), P())
    return jax.shard_map(
        per_device, mesh=mesh, in_specs=placed, out_specs=P(("seq", "blk"), None), check_vma=False
    )
```

```python
import functools
import math

import jax
import jax.numpy as jnp
from jax import lax
from jax.experimental import pallas as pl
from jax.experimental.pallas import tpu as pltpu
from jax.sharding import PartitionSpec as P

HEAD_DIM = 128
MASKED_SCORE = -1e30
CHUNK = 6
EARLY = 4
GROUP = 8
COLLECT_FLOPS = 10**10
FIRST_FLOPS = 10**10
VMEM_BYTES = 40 * 1024 * 1024


def pack_kernel(steps, sources, qkv_ref, *refs):
    outs = refs[len(refs) - len(steps) :]
    groups, _, width = outs[0].shape
    me = lax.axis_index("seq")
    for step, out in zip(steps, outs):
        for group in range(groups):
            start = pl.multiple_of((group * sources + (me ^ step)) * width, width)
            out[group] = qkv_ref[:, pl.ds(start, width)]


def merge_kernel(count, blk_count, tiles_dev, *refs):
    pieces, (cur_ref, kept_list_ref, kept_count_ref) = refs[:count], refs[count : count + 3]
    merged_ref, lists_ref = refs[-2:]
    for i in range(count):
        merged_ref[i] = pieces[i][...]
    me = lax.axis_index("seq")
    region = lax.axis_index("blk")
    for at in range(lists_ref.shape[0]):
        step, place = at // tiles_dev, at % tiles_dev
        tile = ((me ^ step) * blk_count + region) * tiles_dev + place
        near = [cur_ref[c, tile] for c in range(cur_ref.shape[0])]
        entries = [other // (tiles_dev * blk_count) ^ me for other in near]
        entries += [other % tiles_dev for other in near]
        entries += [kept_list_ref[w, tile] for w in range(kept_list_ref.shape[0])]
        entries.append(kept_count_ref[0, tile])
        for i, entry in enumerate(entries):
            lists_ref[at, i : i + 1] = jnp.full((1, lists_ref.shape[2]), entry, jnp.int32)


def collect_kernel(order, *refs):
    for step, span in zip(order, refs):
        refs[-1][step] = span[1:]


def order_kernel(blk_count, *refs):
    kepts, kept_ref = refs[:-1], refs[-1]
    region = lax.axis_index("blk")
    kept_dev = kept_ref.shape[0] // blk_count
    pieces = []
    for ref in kepts:
        pieces += [ref] if len(ref.shape) == 4 else [ref.at[i] for i in range(ref.shape[0])]
    for piece, step in zip(pieces, [*range(0, blk_count, 2), *range(1, blk_count, 2)]):
        kept_ref[pl.ds((region ^ step) * kept_dev, kept_dev)] = piece[...]


def relay_kernel(passed_ref, *refs):
    count = len(refs) // 2
    for i in range(count):
        refs[count + i][0] = refs[i][...]
        refs[count + i][1] = passed_ref[1 + i]


def write_columns(tiles, out_ref, sems):
    me = lax.axis_index("seq")
    copies = []
    for i, (step, tile) in enumerate(tiles):
        width = tile.shape[1]
        columns = pl.ds(pl.multiple_of((me ^ step) * width, width), width)
        copies.append(pltpu.make_async_copy(tile, out_ref.at[:, columns], sems.at[i]))
        copies[-1].start()
    for copy in copies:
        copy.wait()


def first_kernel(direct, passed_ref, *refs):
    tiles = [(1, passed_ref.at[0]), *zip(direct, refs[:-2])]
    write_columns(tiles, refs[-2], refs[-1])


def last_kernel(paired, begun_ref, *refs):
    tiles = []
    for step, ref in zip(paired, refs[:-2]):
        tiles += [(step, ref.at[0]), (step + 1, ref.at[1])]
    write_columns(tiles, refs[-2], refs[-1])


def stack(pieces):
    return jnp.concatenate(pieces, axis=0)


def attend(items, lists_ref, query_refs, span_ref, kept_ref, out_refs, scratch, near_count, window):
    scores, tops_ref, totals_ref, mixed_ref = scratch
    tile_len = scores.shape[1]
    factor = math.log2(math.e) / math.sqrt(HEAD_DIM)
    first = range(min(CHUNK, window))
    later = [range(i, min(i + CHUNK, window)) for i in range(CHUNK, window, CHUNK)]

    def dot_keys(queries, keys):
        raw = lax.dot_general(
            queries, keys, (((1,), (1,)), ((), ())), preferred_element_type=jnp.float32
        )
        return [raw[:, i : i + tile_len] for i in range(0, raw.shape[1], tile_len)]

    def masked(raws, slots, count):
        return [r if w == 0 else jnp.where(w < count, r, MASKED_SCORE) for w, r in zip(slots, raws)]

    def queries_of(u):
        step, rows, cols = items[u][:3]
        return query_refs[step][0, rows, cols]

    def far_blocks(u, kind, slots):
        _, _, cols, _, _, (at, far) = items[u]
        ids = [far[w] if w in far else lists_ref[at, 2 * near_count + w, 0] for w in slots]
        return [kept_ref[i, kind, :, cols] for i in ids]

    def near_blocks(u, kind):
        _, _, cols, _, near, _ = items[u]
        return [span_ref[s, kind, r, cols] for s, r in near]

    def store(u, start, raws):
        for i, r in enumerate(raws):
            scores[u, :, (start + i) * tile_len : (start + i + 1) * tile_len] = r

    def weigh(u, start, top, values):
        weights = []
        for i in range(len(values)):
            r = scores[u, :, (start + i) * tile_len : (start + i + 1) * tile_len]
            weights.append(jnp.exp2(r * factor - top))
        rounded = jnp.concatenate([w.astype(jnp.bfloat16) for w in weights], axis=1)
        mixed = jnp.dot(rounded, stack(values), preferred_element_type=jnp.float32)
        return functools.reduce(jnp.add, weights), mixed

    for u, (_, _, _, count, _, _) in enumerate(items):
        raws = dot_keys(queries_of(u), stack(near_blocks(u, 0) + far_blocks(u, 0, first)))
        raws = raws[:near_count] + masked(raws[near_count:], first, count)
        store(u, 0, raws)
        tops_ref[u] = functools.reduce(jnp.maximum, raws)
    for u, (_, _, _, count, _, _) in enumerate(items):
        for slots in later:

            @pl.when(slots[0] < count)
            def _(u=u, slots=slots, count=count):
                raws = dot_keys(queries_of(u), stack(far_blocks(u, 0, slots)))
                raws = masked(raws, slots, count)
                store(u, near_count + slots[0], raws)
                tops_ref[u] = functools.reduce(jnp.maximum, [tops_ref[u], *raws])

    tops = []
    for u in range(len(items)):
        top = jnp.max(tops_ref[u], axis=1, keepdims=True) * factor
        tops_ref[u] = jnp.broadcast_to(top, tops_ref.shape[1:])
        tops.append(top)
    for u in range(len(items)):
        total, mixed = weigh(u, 0, tops[u], near_blocks(u, 1) + far_blocks(u, 1, first))
        totals_ref[u], mixed_ref[u] = total, mixed
    for u, (_, _, _, count, _, _) in enumerate(items):
        for slots in later:

            @pl.when(slots[0] < count)
            def _(u=u, slots=slots):
                values = far_blocks(u, 1, slots)
                total, mixed = weigh(u, near_count + slots[0], tops_ref[u], values)
                totals_ref[u] += total
                mixed_ref[u] += mixed

    for u, (step, rows, cols, _, _, _) in enumerate(items):
        total = jnp.sum(totals_ref[u], axis=1, keepdims=True)
        out_refs[step][rows, cols] = (mixed_ref[u] / total).astype(jnp.bfloat16)


def attention_kernel(places, tile_len, near_count, window, lists_ref, span_ref, kept_ref, *refs):
    sources = span_ref.shape[0]
    query_refs, buffers, scratch = refs[:sources], refs[sources:-4], refs[-4:]
    out_refs = [buffers[i] if j is None else buffers[i].at[j] for i, j in places]
    _, _, tok_rows, width = span_ref.shape
    tiles_dev = tok_rows // tile_len
    items = []
    for at in range(sources * tiles_dev):
        step, place = at // tiles_dev, at % tiles_dev
        rows = slice(place * tile_len, (place + 1) * tile_len)
        near = []
        for c in range(near_count):
            other_rows = rows
            if tiles_dev > 1:
                start = pl.multiple_of(lists_ref[at, near_count + c, 0] * tile_len, tile_len)
                other_rows = pl.ds(start, tile_len)
            near.append((lists_ref[at, c, 0], other_rows))
        far = {w: lists_ref[at, 2 * near_count + w, 0] for w in range(min(CHUNK, window))}
        count = lists_ref[at, 2 * near_count + window, 0]
        for head in range(width // HEAD_DIM):
            cols = slice(head * HEAD_DIM, (head + 1) * HEAD_DIM)
            items.append((step, rows, cols, count, near, (at, far)))

    for start in range(0, len(items), GROUP):
        attend(
            items[start : start + GROUP],
            lists_ref,
            query_refs,
            span_ref,
            kept_ref,
            out_refs,
            scratch,
            near_count,
            window,
        )


def swap(array, axis, step):
    if step == 0:
        return array
    count = lax.axis_size(axis)
    return lax.ppermute(array, axis, [(i, i ^ step) for i in range(count)])


def sending_order(count):
    near, far = list(range(1, count // 2)), list(range(count // 2, count))
    return near[:1] + far[:1] + near[1:2] + far[1:2] + near[2:] + far[2:]


def per_device(qkv, kept_kv, cur_list, kept_list, kept_count):
    seq_count = lax.axis_size("seq")
    blk_count = lax.axis_size("blk")
    tok_rows = qkv.shape[0]
    kept_dev, _, tile_len, width = kept_kv.shape
    dtype = qkv.dtype
    near_count, window = cur_list.shape[1], kept_list.shape[1]
    vmem = pl.BlockSpec(memory_space=pltpu.VMEM)
    anywhere = pl.BlockSpec(memory_space=pl.ANY)
    smem = pl.BlockSpec(memory_space=pltpu.SMEM)
    params = pltpu.CompilerParams(vmem_limit_bytes=VMEM_BYTES)

    kepts = [swap(kept_kv, "blk", step) for step in range(0, blk_count, 2)]
    order = sending_order(seq_count)
    spans = [None] * seq_count
    for steps in ([0, *order[:EARLY]], order[EARLY:]):
        before = [] if 0 in steps else [*kepts[1:], spans[order[0]]]
        packed = pl.pallas_call(
            functools.partial(pack_kernel, steps, seq_count),
            out_shape=[jax.ShapeDtypeStruct((3, tok_rows, width), dtype)] * len(steps),
            in_specs=[vmem] + [anywhere] * len(before),
            out_specs=[vmem] * len(steps),
            compiler_params=params,
            name="pack",
        )(qkv, *before)
        for step, piece in zip(steps, packed):
            spans[step] = swap(piece, "seq", step)
    after = []
    tiles_dev = tok_rows // tile_len
    merged, lists = pl.pallas_call(
        functools.partial(merge_kernel, len(kepts), blk_count, tiles_dev),
        out_shape=[
            jax.ShapeDtypeStruct((len(kepts), *kept_kv.shape), dtype),
            jax.ShapeDtypeStruct(
                (seq_count * tiles_dev, 2 * near_count + window + 1, HEAD_DIM), jnp.int32
            ),
        ],
        in_specs=[vmem] * len(kepts) + [smem] * 3,
        out_specs=[vmem] * 2,
        compiler_params=params,
        name="merge",
    )(*kepts, cur_list.T, kept_list.T, kept_count[None])
    kepts.append(swap(merged, "blk", 1))

    kept = pl.pallas_call(
        functools.partial(order_kernel, blk_count),
        out_shape=jax.ShapeDtypeStruct((blk_count * kept_dev, 2, tile_len, width), dtype),
        in_specs=[vmem] * len(kepts),
        out_specs=vmem,
        compiler_params=params,
        name="order",
    )(*kepts)
    span = pl.pallas_call(
        functools.partial(collect_kernel, [0, *order]),
        out_shape=jax.ShapeDtypeStruct((seq_count, 2, tok_rows, width), dtype),
        in_specs=[vmem] * seq_count,
        out_specs=vmem,
        compiler_params=params,
        cost_estimate=pl.CostEstimate(flops=COLLECT_FLOPS, bytes_accessed=0, transcendentals=0),
        name="collect",
    )(*[spans[step] for step in [0, *order]])

    half = seq_count // 2
    direct = [0, half + 1, half]
    paired = [step for step in range(seq_count - 2, 0, -2) if step != half]
    passed = [1] + [step + 1 for step in paired]
    places = [None] * seq_count
    for i, step in enumerate(direct + paired):
        places[step] = (1 + i, None)
    for i, step in enumerate(passed):
        places[step] = (0, i)
    one = jax.ShapeDtypeStruct((tok_rows, width), dtype)
    two = jax.ShapeDtypeStruct((2, tok_rows, width), dtype)
    per_step = tok_rows // tile_len * (width // HEAD_DIM)
    group = min(GROUP, seq_count * per_step)
    sent, *outs = pl.pallas_call(
        functools.partial(attention_kernel, places, tile_len, near_count, window),
        out_shape=[jax.ShapeDtypeStruct((len(passed), tok_rows, width), dtype)]
        + [one] * len(direct + paired),
        in_specs=[vmem] * (3 + seq_count),
        out_specs=[vmem] * (1 + len(direct + paired)),
        scratch_shapes=[
            pltpu.VMEM((group, tile_len, (near_count + window) * tile_len), jnp.float32),
            *[pltpu.VMEM((group, tile_len, tile_len), jnp.float32)] * 3,
        ],
        compiler_params=params,
        name="attention",
    )(lists, span, kept, *spans)

    sent = swap(sent, "seq", 1)
    outs = outs[:1] + [swap(out, "seq", step) for out, step in zip(outs[1:], direct[1:])] + outs[len(direct):]
    relayed = pl.pallas_call(
        relay_kernel,
        out_shape=[two] * len(paired),
        in_specs=[vmem] * (1 + len(paired)),
        out_specs=[vmem] * len(paired),
        compiler_params=params,
        name="relay",
    )(sent, *outs[len(direct):])
    relayed = [swap(buffer, "seq", step) for buffer, step in zip(relayed, paired)]
    whole = jax.ShapeDtypeStruct((tok_rows, seq_count * width), dtype)
    begun = pl.pallas_call(
        functools.partial(first_kernel, direct),
        out_shape=whole,
        in_specs=[vmem] * (1 + len(direct)),
        out_specs=anywhere,
        scratch_shapes=[pltpu.SemaphoreType.DMA((1 + len(direct),))],
        compiler_params=params,
        cost_estimate=pl.CostEstimate(flops=FIRST_FLOPS, bytes_accessed=0, transcendentals=0),
        name="first",
    )(sent, *outs[: len(direct)])
    return pl.pallas_call(
        functools.partial(last_kernel, paired),
        out_shape=whole,
        in_specs=[anywhere] + [vmem] * len(paired),
        out_specs=anywhere,
        scratch_shapes=[pltpu.SemaphoreType.DMA((2 * len(paired),))],
        compiler_params=params,
        input_output_aliases={0: 0},
        name="last",
    )(begun, *relayed)


def solution(mesh):
    placed = (P(("seq", "blk"), None), P("blk", None, None, "seq"), P(), P(), P())
    return jax.shard_map(
        per_device, mesh=mesh, in_specs=placed, out_specs=P(("seq", "blk"), None), check_vma=False
    )
```

```python
import functools
import math

import jax
import jax.numpy as jnp
from jax import lax
from jax.experimental import pallas as pl
from jax.experimental.pallas import tpu as pltpu
from jax.sharding import PartitionSpec as P

HEAD_DIM = 128
MASKED_SCORE = -1e30
CHUNK = 8
EARLY = 4
GROUP = 8
COLLECT_FLOPS = 10**10
FIRST_FLOPS = 10**10
VMEM_BYTES = 40 * 1024 * 1024


def pack_kernel(steps, sources, qkv_ref, *refs):
    outs = refs[len(refs) - len(steps) :]
    groups, _, width = outs[0].shape
    me = lax.axis_index("seq")
    for step, out in zip(steps, outs):
        for group in range(groups):
            start = pl.multiple_of((group * sources + (me ^ step)) * width, width)
            out[group] = qkv_ref[:, pl.ds(start, width)]


def merge_kernel(count, blk_count, tiles_dev, *refs):
    pieces, (cur_ref, kept_list_ref, kept_count_ref) = refs[:count], refs[count : count + 3]
    merged_ref, lists_ref = refs[-2:]
    for i in range(count):
        merged_ref[i] = pieces[i][...]
    me = lax.axis_index("seq")
    region = lax.axis_index("blk")
    for at in range(lists_ref.shape[0]):
        step, place = at // tiles_dev, at % tiles_dev
        tile = ((me ^ step) * blk_count + region) * tiles_dev + place
        near = [cur_ref[c, tile] for c in range(cur_ref.shape[0])]
        entries = [other // (tiles_dev * blk_count) ^ me for other in near]
        entries += [other % tiles_dev for other in near]
        entries += [kept_list_ref[w, tile] for w in range(kept_list_ref.shape[0])]
        entries.append(kept_count_ref[0, tile])
        for i, entry in enumerate(entries):
            lists_ref[at, i : i + 1] = jnp.full((1, lists_ref.shape[2]), entry, jnp.int32)


def collect_kernel(order, *refs):
    for step, span in zip(order, refs):
        refs[-1][step] = span[1:]


def order_kernel(blk_count, *refs):
    kepts, kept_ref = refs[:-1], refs[-1]
    region = lax.axis_index("blk")
    kept_dev = kept_ref.shape[0] // blk_count
    pieces = []
    for ref in kepts:
        pieces += [ref] if len(ref.shape) == 4 else [ref.at[i] for i in range(ref.shape[0])]
    for piece, step in zip(pieces, [*range(0, blk_count, 2), *range(1, blk_count, 2)]):
        kept_ref[pl.ds((region ^ step) * kept_dev, kept_dev)] = piece[...]


def relay_kernel(passed_ref, *refs):
    count = len(refs) // 2
    for i in range(count):
        refs[count + i][0] = refs[i][...]
        refs[count + i][1] = passed_ref[1 + i]


def write_columns(tiles, out_ref, sems):
    me = lax.axis_index("seq")
    copies = []
    for i, (step, tile) in enumerate(tiles):
        width = tile.shape[1]
        columns = pl.ds(pl.multiple_of((me ^ step) * width, width), width)
        copies.append(pltpu.make_async_copy(tile, out_ref.at[:, columns], sems.at[i]))
        copies[-1].start()
    for copy in copies:
        copy.wait()


def first_kernel(direct, passed_ref, *refs):
    tiles = [(1, passed_ref.at[0]), *zip(direct, refs[:-2])]
    write_columns(tiles, refs[-2], refs[-1])


def last_kernel(paired, begun_ref, *refs):
    tiles = []
    for step, ref in zip(paired, refs[:-2]):
        tiles += [(step, ref.at[0]), (step + 1, ref.at[1])]
    write_columns(tiles, refs[-2], refs[-1])


def stack(pieces):
    return jnp.concatenate(pieces, axis=0)


def attend(items, query_refs, span_ref, kept_ref, out_refs, scratch, near_count, window):
    scores, tops_ref, totals_ref, mixed_ref = scratch
    tile_len = scores.shape[1]
    factor = math.log2(math.e) / math.sqrt(HEAD_DIM)
    first = range(min(CHUNK, window))
    later = [range(i, min(i + CHUNK, window)) for i in range(CHUNK, window, CHUNK)]

    def dot_keys(queries, keys):
        raw = lax.dot_general(
            queries, keys, (((1,), (1,)), ((), ())), preferred_element_type=jnp.float32
        )
        return [raw[:, i : i + tile_len] for i in range(0, raw.shape[1], tile_len)]

    def masked(raws, slots, count):
        return [r if w == 0 else jnp.where(w < count, r, MASKED_SCORE) for w, r in zip(slots, raws)]

    def queries_of(u):
        step, rows, cols = items[u][:3]
        return query_refs[step][0, rows, cols]

    def far_blocks(u, kind, slots):
        _, _, cols, _, _, far = items[u]
        return [kept_ref[far[w], kind, :, cols] for w in slots]

    def near_blocks(u, kind):
        _, _, cols, _, near, _ = items[u]
        return [span_ref[s, kind, r, cols] for s, r in near]

    def store(u, start, raws):
        for i, r in enumerate(raws):
            scores[u, :, (start + i) * tile_len : (start + i + 1) * tile_len] = r

    def weigh(u, start, top, values):
        weights = []
        for i in range(len(values)):
            r = scores[u, :, (start + i) * tile_len : (start + i + 1) * tile_len]
            weights.append(jnp.exp2(r * factor - top))
        rounded = jnp.concatenate([w.astype(jnp.bfloat16) for w in weights], axis=1)
        mixed = jnp.dot(rounded, stack(values), preferred_element_type=jnp.float32)
        return functools.reduce(jnp.add, weights), mixed

    for u, (_, _, _, count, _, _) in enumerate(items):
        raws = dot_keys(queries_of(u), stack(near_blocks(u, 0) + far_blocks(u, 0, first)))
        raws = raws[:near_count] + masked(raws[near_count:], first, count)
        store(u, 0, raws)
        tops_ref[u] = functools.reduce(jnp.maximum, raws)
    for u, (_, _, _, count, _, _) in enumerate(items):
        for slots in later:

            @pl.when(slots[0] < count)
            def _(u=u, slots=slots, count=count):
                raws = dot_keys(queries_of(u), stack(far_blocks(u, 0, slots)))
                raws = masked(raws, slots, count)
                store(u, near_count + slots[0], raws)
                tops_ref[u] = functools.reduce(jnp.maximum, [tops_ref[u], *raws])

    tops = []
    for u in range(len(items)):
        top = jnp.max(tops_ref[u], axis=1, keepdims=True) * factor
        tops_ref[u] = jnp.broadcast_to(top, tops_ref.shape[1:])
        tops.append(top)
    for u in range(len(items)):
        total, mixed = weigh(u, 0, tops[u], near_blocks(u, 1) + far_blocks(u, 1, first))
        totals_ref[u], mixed_ref[u] = total, mixed
    for u, (_, _, _, count, _, _) in enumerate(items):
        for slots in later:

            @pl.when(slots[0] < count)
            def _(u=u, slots=slots):
                values = far_blocks(u, 1, slots)
                total, mixed = weigh(u, near_count + slots[0], tops_ref[u], values)
                totals_ref[u] += total
                mixed_ref[u] += mixed

    for u, (step, rows, cols, _, _, _) in enumerate(items):
        total = jnp.sum(totals_ref[u], axis=1, keepdims=True)
        out_refs[step][rows, cols] = (mixed_ref[u] / total).astype(jnp.bfloat16)


def attention_kernel(places, tile_len, near_count, window, lists_ref, span_ref, kept_ref, *refs):
    sources = span_ref.shape[0]
    query_refs, buffers, scratch = refs[:sources], refs[sources:-4], refs[-4:]
    out_refs = [buffers[i] if j is None else buffers[i].at[j] for i, j in places]
    _, _, tok_rows, width = span_ref.shape
    tiles_dev = tok_rows // tile_len
    items = []
    for at in range(sources * tiles_dev):
        step, place = at // tiles_dev, at % tiles_dev
        rows = slice(place * tile_len, (place + 1) * tile_len)
        near = []
        for c in range(near_count):
            start = pl.multiple_of(lists_ref[at, near_count + c, 0] * tile_len, tile_len)
            near.append((lists_ref[at, c, 0], pl.ds(start, tile_len)))
        far = [lists_ref[at, 2 * near_count + w, 0] for w in range(window)]
        count = lists_ref[at, 2 * near_count + window, 0]
        for head in range(width // HEAD_DIM):
            cols = slice(head * HEAD_DIM, (head + 1) * HEAD_DIM)
            items.append((step, rows, cols, count, near, far))

    for start in range(0, len(items), GROUP):
        attend(
            items[start : start + GROUP],
            query_refs,
            span_ref,
            kept_ref,
            out_refs,
            scratch,
            near_count,
            window,
        )


def swap(array, axis, step):
    if step == 0:
        return array
    count = lax.axis_size(axis)
    return lax.ppermute(array, axis, [(i, i ^ step) for i in range(count)])


def sending_order(count):
    near, far = list(range(1, count // 2)), list(range(count // 2, count))
    return near[:1] + far[:1] + near[1:2] + far[1:2] + near[2:] + far[2:]


def per_device(qkv, kept_kv, cur_list, kept_list, kept_count):
    seq_count = lax.axis_size("seq")
    blk_count = lax.axis_size("blk")
    tok_rows = qkv.shape[0]
    kept_dev, _, tile_len, width = kept_kv.shape
    dtype = qkv.dtype
    near_count, window = cur_list.shape[1], kept_list.shape[1]
    vmem = pl.BlockSpec(memory_space=pltpu.VMEM)
    anywhere = pl.BlockSpec(memory_space=pl.ANY)
    smem = pl.BlockSpec(memory_space=pltpu.SMEM)
    params = pltpu.CompilerParams(vmem_limit_bytes=VMEM_BYTES)

    kepts = [swap(kept_kv, "blk", step) for step in range(0, blk_count, 2)]
    order = sending_order(seq_count)
    spans = [None] * seq_count
    for steps in ([0, *order[:EARLY]], order[EARLY:]):
        before = [] if 0 in steps else [*kepts[1:], spans[order[0]]]
        packed = pl.pallas_call(
            functools.partial(pack_kernel, steps, seq_count),
            out_shape=[jax.ShapeDtypeStruct((3, tok_rows, width), dtype)] * len(steps),
            in_specs=[vmem] + [anywhere] * len(before),
            out_specs=[vmem] * len(steps),
            compiler_params=params,
            name="pack",
        )(qkv, *before)
        for step, piece in zip(steps, packed):
            spans[step] = swap(piece, "seq", step)
    after = []
    tiles_dev = tok_rows // tile_len
    merged, lists = pl.pallas_call(
        functools.partial(merge_kernel, len(kepts), blk_count, tiles_dev),
        out_shape=[
            jax.ShapeDtypeStruct((len(kepts), *kept_kv.shape), dtype),
            jax.ShapeDtypeStruct(
                (seq_count * tiles_dev, 2 * near_count + window + 1, HEAD_DIM), jnp.int32
            ),
        ],
        in_specs=[vmem] * len(kepts) + [smem] * 3,
        out_specs=[vmem] * 2,
        compiler_params=params,
        name="merge",
    )(*kepts, cur_list.T, kept_list.T, kept_count[None])
    kepts.append(swap(merged, "blk", 1))

    kept = pl.pallas_call(
        functools.partial(order_kernel, blk_count),
        out_shape=jax.ShapeDtypeStruct((blk_count * kept_dev, 2, tile_len, width), dtype),
        in_specs=[vmem] * len(kepts),
        out_specs=vmem,
        compiler_params=params,
        name="order",
    )(*kepts)
    span = pl.pallas_call(
        functools.partial(collect_kernel, [0, *order]),
        out_shape=jax.ShapeDtypeStruct((seq_count, 2, tok_rows, width), dtype),
        in_specs=[vmem] * seq_count,
        out_specs=vmem,
        compiler_params=params,
        cost_estimate=pl.CostEstimate(flops=COLLECT_FLOPS, bytes_accessed=0, transcendentals=0),
        name="collect",
    )(*[spans[step] for step in [0, *order]])

    half = seq_count // 2
    direct = [0, half + 1, half]
    paired = [step for step in range(seq_count - 2, 0, -2) if step != half]
    passed = [1] + [step + 1 for step in paired]
    places = [None] * seq_count
    for i, step in enumerate(direct + paired):
        places[step] = (1 + i, None)
    for i, step in enumerate(passed):
        places[step] = (0, i)
    one = jax.ShapeDtypeStruct((tok_rows, width), dtype)
    two = jax.ShapeDtypeStruct((2, tok_rows, width), dtype)
    per_step = tok_rows // tile_len * (width // HEAD_DIM)
    group = min(GROUP, seq_count * per_step)
    sent, *outs = pl.pallas_call(
        functools.partial(attention_kernel, places, tile_len, near_count, window),
        out_shape=[jax.ShapeDtypeStruct((len(passed), tok_rows, width), dtype)]
        + [one] * len(direct + paired),
        in_specs=[vmem] * (3 + seq_count),
        out_specs=[vmem] * (1 + len(direct + paired)),
        scratch_shapes=[
            pltpu.VMEM((group, tile_len, (near_count + window) * tile_len), jnp.float32),
            *[pltpu.VMEM((group, tile_len, tile_len), jnp.float32)] * 3,
        ],
        compiler_params=params,
        name="attention",
    )(lists, span, kept, *spans)

    sent = swap(sent, "seq", 1)
    outs = outs[:1] + [swap(out, "seq", step) for out, step in zip(outs[1:], direct[1:])] + outs[len(direct):]
    relayed = pl.pallas_call(
        relay_kernel,
        out_shape=[two] * len(paired),
        in_specs=[vmem] * (1 + len(paired)),
        out_specs=[vmem] * len(paired),
        compiler_params=params,
        name="relay",
    )(sent, *outs[len(direct):])
    relayed = [swap(buffer, "seq", step) for buffer, step in zip(relayed, paired)]
    whole = jax.ShapeDtypeStruct((tok_rows, seq_count * width), dtype)
    begun = pl.pallas_call(
        functools.partial(first_kernel, direct),
        out_shape=whole,
        in_specs=[vmem] * (1 + len(direct)),
        out_specs=anywhere,
        scratch_shapes=[pltpu.SemaphoreType.DMA((1 + len(direct),))],
        compiler_params=params,
        cost_estimate=pl.CostEstimate(flops=FIRST_FLOPS, bytes_accessed=0, transcendentals=0),
        name="first",
    )(sent, *outs[: len(direct)])
    return pl.pallas_call(
        functools.partial(last_kernel, paired),
        out_shape=whole,
        in_specs=[anywhere] + [vmem] * len(paired),
        out_specs=anywhere,
        scratch_shapes=[pltpu.SemaphoreType.DMA((2 * len(paired),))],
        compiler_params=params,
        input_output_aliases={0: 0},
        name="last",
    )(begun, *relayed)


def solution(mesh):
    placed = (P(("seq", "blk"), None), P("blk", None, None, "seq"), P(), P(), P())
    return jax.shard_map(
        per_device, mesh=mesh, in_specs=placed, out_specs=P(("seq", "blk"), None), check_vma=False
    )
```

```python
import functools
import math

import jax
import jax.numpy as jnp
from jax import lax
from jax.experimental import pallas as pl
from jax.experimental.pallas import tpu as pltpu
from jax.sharding import PartitionSpec as P

HEAD_DIM = 128
MASKED_SCORE = -1e30
CHUNK = 7
EARLY = 4
GROUP = 8
COLLECT_FLOPS = 10**10
FIRST_FLOPS = 10**10
VMEM_BYTES = 40 * 1024 * 1024


def pack_kernel(steps, sources, qkv_ref, *refs):
    outs = refs[len(refs) - len(steps) :]
    groups, _, width = outs[0].shape
    me = lax.axis_index("seq")
    for step, out in zip(steps, outs):
        for group in range(groups):
            start = pl.multiple_of((group * sources + (me ^ step)) * width, width)
            out[group] = qkv_ref[:, pl.ds(start, width)]


def merge_kernel(count, blk_count, tiles_dev, *refs):
    pieces, (cur_ref, kept_list_ref, kept_count_ref) = refs[:count], refs[count : count + 3]
    merged_ref, lists_ref = refs[-2:]
    for i in range(count):
        merged_ref[i] = pieces[i][...]
    me = lax.axis_index("seq")
    region = lax.axis_index("blk")
    for at in range(lists_ref.shape[0]):
        step, place = at // tiles_dev, at % tiles_dev
        tile = ((me ^ step) * blk_count + region) * tiles_dev + place
        near = [cur_ref[c, tile] for c in range(cur_ref.shape[0])]
        entries = [other // (tiles_dev * blk_count) ^ me for other in near]
        entries += [other % tiles_dev for other in near]
        entries += [kept_list_ref[w, tile] for w in range(kept_list_ref.shape[0])]
        entries.append(kept_count_ref[0, tile])
        for i, entry in enumerate(entries):
            lists_ref[at, i : i + 1] = jnp.full((1, lists_ref.shape[2]), entry, jnp.int32)


def collect_kernel(order, *refs):
    for step, span in zip(order, refs):
        refs[-1][step] = span[1:]


def order_kernel(blk_count, *refs):
    kepts, kept_ref = refs[:-1], refs[-1]
    region = lax.axis_index("blk")
    kept_dev = kept_ref.shape[0] // blk_count
    pieces = []
    for ref in kepts:
        pieces += [ref] if len(ref.shape) == 4 else [ref.at[i] for i in range(ref.shape[0])]
    for piece, step in zip(pieces, [*range(0, blk_count, 2), *range(1, blk_count, 2)]):
        kept_ref[pl.ds((region ^ step) * kept_dev, kept_dev)] = piece[...]


def relay_kernel(passed_ref, *refs):
    count = len(refs) // 2
    for i in range(count):
        refs[count + i][0] = refs[i][...]
        refs[count + i][1] = passed_ref[1 + i]


def write_columns(tiles, out_ref, sems):
    me = lax.axis_index("seq")
    copies = []
    for i, (step, tile) in enumerate(tiles):
        width = tile.shape[1]
        columns = pl.ds(pl.multiple_of((me ^ step) * width, width), width)
        copies.append(pltpu.make_async_copy(tile, out_ref.at[:, columns], sems.at[i]))
        copies[-1].start()
    for copy in copies:
        copy.wait()


def first_kernel(direct, passed_ref, *refs):
    tiles = [(1, passed_ref.at[0]), *zip(direct, refs[:-2])]
    write_columns(tiles, refs[-2], refs[-1])


def last_kernel(paired, begun_ref, *refs):
    tiles = []
    for step, ref in zip(paired, refs[:-2]):
        tiles += [(step, ref.at[0]), (step + 1, ref.at[1])]
    write_columns(tiles, refs[-2], refs[-1])


def stack(pieces):
    return jnp.concatenate(pieces, axis=0)


def attend(items, query_refs, span_ref, kept_ref, out_refs, scratch, near_count, window):
    scores, tops_ref, totals_ref, mixed_ref = scratch
    tile_len = scores.shape[1]
    factor = math.log2(math.e) / math.sqrt(HEAD_DIM)
    first = range(min(CHUNK, window))
    later = [range(i, min(i + CHUNK, window)) for i in range(CHUNK, window, CHUNK)]

    def dot_keys(queries, keys):
        raw = lax.dot_general(
            queries, keys, (((1,), (1,)), ((), ())), preferred_element_type=jnp.float32
        )
        return [raw[:, i : i + tile_len] for i in range(0, raw.shape[1], tile_len)]

    def masked(raws, slots, count):
        return [r if w == 0 else jnp.where(w < count, r, MASKED_SCORE) for w, r in zip(slots, raws)]

    def queries_of(u):
        step, rows, cols = items[u][:3]
        return query_refs[step][0, rows, cols]

    def far_blocks(u, kind, slots):
        _, _, cols, _, _, far = items[u]
        return [kept_ref[far[w], kind, :, cols] for w in slots]

    def near_blocks(u, kind):
        _, _, cols, _, near, _ = items[u]
        return [span_ref[s, kind, r, cols] for s, r in near]

    def store(u, start, raws):
        for i, r in enumerate(raws):
            scores[u, :, (start + i) * tile_len : (start + i + 1) * tile_len] = r

    def weigh(u, start, top, values):
        weights = []
        for i in range(len(values)):
            r = scores[u, :, (start + i) * tile_len : (start + i + 1) * tile_len]
            weights.append(jnp.exp2(r * factor - top))
        rounded = jnp.concatenate([w.astype(jnp.bfloat16) for w in weights], axis=1)
        mixed = jnp.dot(rounded, stack(values), preferred_element_type=jnp.float32)
        return functools.reduce(jnp.add, weights), mixed

    for u, (_, _, _, count, _, _) in enumerate(items):
        raws = dot_keys(queries_of(u), stack(near_blocks(u, 0) + far_blocks(u, 0, first)))
        raws = raws[:near_count] + masked(raws[near_count:], first, count)
        store(u, 0, raws)
        tops_ref[u] = functools.reduce(jnp.maximum, raws)
    for u, (_, _, _, count, _, _) in enumerate(items):
        for slots in later:

            @pl.when(slots[0] < count)
            def _(u=u, slots=slots, count=count):
                raws = dot_keys(queries_of(u), stack(far_blocks(u, 0, slots)))
                raws = masked(raws, slots, count)
                store(u, near_count + slots[0], raws)
                tops_ref[u] = functools.reduce(jnp.maximum, [tops_ref[u], *raws])

    tops = []
    for u in range(len(items)):
        top = jnp.max(tops_ref[u], axis=1, keepdims=True) * factor
        tops_ref[u] = jnp.broadcast_to(top, tops_ref.shape[1:])
        tops.append(top)
    for u in range(len(items)):
        total, mixed = weigh(u, 0, tops[u], near_blocks(u, 1) + far_blocks(u, 1, first))
        totals_ref[u], mixed_ref[u] = total, mixed
    for u, (_, _, _, count, _, _) in enumerate(items):
        for slots in later:

            @pl.when(slots[0] < count)
            def _(u=u, slots=slots):
                values = far_blocks(u, 1, slots)
                total, mixed = weigh(u, near_count + slots[0], tops_ref[u], values)
                totals_ref[u] += total
                mixed_ref[u] += mixed

    for u, (step, rows, cols, _, _, _) in enumerate(items):
        total = jnp.sum(totals_ref[u], axis=1, keepdims=True)
        out_refs[step][rows, cols] = (mixed_ref[u] / total).astype(jnp.bfloat16)


def attention_kernel(places, tile_len, near_count, window, lists_ref, span_ref, kept_ref, *refs):
    sources = span_ref.shape[0]
    query_refs, buffers, scratch = refs[:sources], refs[sources:-4], refs[-4:]
    out_refs = [buffers[i] if j is None else buffers[i].at[j] for i, j in places]
    _, _, tok_rows, width = span_ref.shape
    tiles_dev = tok_rows // tile_len
    items = []
    for at in range(sources * tiles_dev):
        step, place = at // tiles_dev, at % tiles_dev
        rows = slice(place * tile_len, (place + 1) * tile_len)
        near = []
        for c in range(near_count):
            start = pl.multiple_of(lists_ref[at, near_count + c, 0] * tile_len, tile_len)
            near.append((lists_ref[at, c, 0], pl.ds(start, tile_len)))
        far = [lists_ref[at, 2 * near_count + w, 0] for w in range(window)]
        count = lists_ref[at, 2 * near_count + window, 0]
        for head in range(width // HEAD_DIM):
            cols = slice(head * HEAD_DIM, (head + 1) * HEAD_DIM)
            items.append((step, rows, cols, count, near, far))

    for start in range(0, len(items), GROUP):
        attend(
            items[start : start + GROUP],
            query_refs,
            span_ref,
            kept_ref,
            out_refs,
            scratch,
            near_count,
            window,
        )


def swap(array, axis, step):
    if step == 0:
        return array
    count = lax.axis_size(axis)
    return lax.ppermute(array, axis, [(i, i ^ step) for i in range(count)])


def sending_order(count):
    near, far = list(range(1, count // 2)), list(range(count // 2, count))
    return near[:1] + far[:1] + near[1:2] + far[1:2] + near[2:] + far[2:]


def per_device(qkv, kept_kv, cur_list, kept_list, kept_count):
    seq_count = lax.axis_size("seq")
    blk_count = lax.axis_size("blk")
    tok_rows = qkv.shape[0]
    kept_dev, _, tile_len, width = kept_kv.shape
    dtype = qkv.dtype
    near_count, window = cur_list.shape[1], kept_list.shape[1]
    vmem = pl.BlockSpec(memory_space=pltpu.VMEM)
    anywhere = pl.BlockSpec(memory_space=pl.ANY)
    smem = pl.BlockSpec(memory_space=pltpu.SMEM)
    params = pltpu.CompilerParams(vmem_limit_bytes=VMEM_BYTES)

    kepts = [swap(kept_kv, "blk", step) for step in range(0, blk_count, 2)]
    order = sending_order(seq_count)
    spans = [None] * seq_count
    for steps in ([0, *order[:EARLY]], order[EARLY:]):
        before = [] if 0 in steps else [*kepts[1:], spans[order[0]]]
        packed = pl.pallas_call(
            functools.partial(pack_kernel, steps, seq_count),
            out_shape=[jax.ShapeDtypeStruct((3, tok_rows, width), dtype)] * len(steps),
            in_specs=[vmem] + [anywhere] * len(before),
            out_specs=[vmem] * len(steps),
            compiler_params=params,
            name="pack",
        )(qkv, *before)
        for step, piece in zip(steps, packed):
            spans[step] = swap(piece, "seq", step)
    after = []
    tiles_dev = tok_rows // tile_len
    merged, lists = pl.pallas_call(
        functools.partial(merge_kernel, len(kepts), blk_count, tiles_dev),
        out_shape=[
            jax.ShapeDtypeStruct((len(kepts), *kept_kv.shape), dtype),
            jax.ShapeDtypeStruct(
                (seq_count * tiles_dev, 2 * near_count + window + 1, HEAD_DIM), jnp.int32
            ),
        ],
        in_specs=[vmem] * len(kepts) + [smem] * 3,
        out_specs=[vmem] * 2,
        compiler_params=params,
        name="merge",
    )(*kepts, cur_list.T, kept_list.T, kept_count[None])
    kepts.append(swap(merged, "blk", 1))

    kept = pl.pallas_call(
        functools.partial(order_kernel, blk_count),
        out_shape=jax.ShapeDtypeStruct((blk_count * kept_dev, 2, tile_len, width), dtype),
        in_specs=[vmem] * len(kepts),
        out_specs=vmem,
        compiler_params=params,
        name="order",
    )(*kepts)
    span = pl.pallas_call(
        functools.partial(collect_kernel, [0, *order]),
        out_shape=jax.ShapeDtypeStruct((seq_count, 2, tok_rows, width), dtype),
        in_specs=[vmem] * seq_count,
        out_specs=vmem,
        compiler_params=params,
        cost_estimate=pl.CostEstimate(flops=COLLECT_FLOPS, bytes_accessed=0, transcendentals=0),
        name="collect",
    )(*[spans[step] for step in [0, *order]])

    half = seq_count // 2
    direct = [0, half + 1, half]
    paired = [step for step in range(seq_count - 2, 0, -2) if step != half]
    passed = [1] + [step + 1 for step in paired]
    places = [None] * seq_count
    for i, step in enumerate(direct + paired):
        places[step] = (1 + i, None)
    for i, step in enumerate(passed):
        places[step] = (0, i)
    one = jax.ShapeDtypeStruct((tok_rows, width), dtype)
    two = jax.ShapeDtypeStruct((2, tok_rows, width), dtype)
    per_step = tok_rows // tile_len * (width // HEAD_DIM)
    group = min(GROUP, seq_count * per_step)
    sent, *outs = pl.pallas_call(
        functools.partial(attention_kernel, places, tile_len, near_count, window),
        out_shape=[jax.ShapeDtypeStruct((len(passed), tok_rows, width), dtype)]
        + [one] * len(direct + paired),
        in_specs=[vmem] * (3 + seq_count),
        out_specs=[vmem] * (1 + len(direct + paired)),
        scratch_shapes=[
            pltpu.VMEM((group, tile_len, (near_count + window) * tile_len), jnp.float32),
            *[pltpu.VMEM((group, tile_len, tile_len), jnp.float32)] * 3,
        ],
        compiler_params=params,
        name="attention",
    )(lists, span, kept, *spans)

    sent = swap(sent, "seq", 1)
    outs = outs[:1] + [swap(out, "seq", step) for out, step in zip(outs[1:], direct[1:])] + outs[len(direct):]
    relayed = pl.pallas_call(
        relay_kernel,
        out_shape=[two] * len(paired),
        in_specs=[vmem] * (1 + len(paired)),
        out_specs=[vmem] * len(paired),
        compiler_params=params,
        name="relay",
    )(sent, *outs[len(direct):])
    relayed = [swap(buffer, "seq", step) for buffer, step in zip(relayed, paired)]
    whole = jax.ShapeDtypeStruct((tok_rows, seq_count * width), dtype)
    begun = pl.pallas_call(
        functools.partial(first_kernel, direct),
        out_shape=whole,
        in_specs=[vmem] * (1 + len(direct)),
        out_specs=anywhere,
        scratch_shapes=[pltpu.SemaphoreType.DMA((1 + len(direct),))],
        compiler_params=params,
        cost_estimate=pl.CostEstimate(flops=FIRST_FLOPS, bytes_accessed=0, transcendentals=0),
        name="first",
    )(sent, *outs[: len(direct)])
    return pl.pallas_call(
        functools.partial(last_kernel, paired),
        out_shape=whole,
        in_specs=[anywhere] + [vmem] * len(paired),
        out_specs=anywhere,
        scratch_shapes=[pltpu.SemaphoreType.DMA((2 * len(paired),))],
        compiler_params=params,
        input_output_aliases={0: 0},
        name="last",
    )(begun, *relayed)


def solution(mesh):
    placed = (P(("seq", "blk"), None), P("blk", None, None, "seq"), P(), P(), P())
    return jax.shard_map(
        per_device, mesh=mesh, in_specs=placed, out_specs=P(("seq", "blk"), None), check_vma=False
    )
```
